32 devices in a mesh: section: 4 (over y, x), tile: 8 (over z, core).
Axes of the slice: x: 2, y: 2, z: 4, core: 2. Of those that a mesh axis runs over, the one named last changes fastest.
Arguments:
- inputs: bfloat16 [4, 8, 16, 1024], P(None, 'tile'), may hold values from -40 to 40
- cotangent: bfloat16 [4, 8, 16, 1024], P(None, 'tile'), may hold values from -6 to 6
- depth_weight: bfloat16 [8, 49, 64], P('section'), may hold values from -0.875 to 0.875
- in_weight: bfloat16 [8, 64, 256], P('section'), may hold values from -0.75 to 0.75
- out_weight: bfloat16 [8, 256, 64], P('section'), may hold values from -0.375 to 0.375
- neighbours: int32 [8, 8], P('tile'), may hold values from -1 to 7, as said below
- orientation: int32 [8], replicated, may hold values from 0 to 3, as said below
Outputs:
- section_outputs: bfloat16 [4, 4, 8, 16, 1024], P('section', None, 'tile')
- section_grads: bfloat16 [4, 4, 8, 16, 1024], P('section', None, 'tile')
- depth_grads: float32 [8, 49, 64], P('section')
- in_grads: float32 [8, 64, 256], P('section')
- out_grads: float32 [8, 256, 64], P('section')
The draws below stay inside these ranges and needn't reach their ends.
Inputs may be any that keep to these rules, and one draw needn't show every extreme that they name: Tile t stores its pixels turned by orientation[t] quarter turns counterclockwise. The tiles form a grid of 4 columns numbered row by row, the numbering closing on itself modulo 8. For local direction k (0 to 3: north, east, south, west; 4 to 7: north-east, south-east, south-west, north-west) the true direction is j = 4 * (k // 4) + (k + orientation[t]) mod 4, and neighbours[t, k] = (t + d_j) mod 8 with d_j = -4, 1, 4, -1, 1 - 4, 5, 3, -4 - 1 for j = 0..7, except that a corner entry is -1 where no tile meets that vertex; if tile t's true north-east corner is -1, so is the true south-west corner of tile (t - 3) mod 8, and no other corner is -1. `orientation`: tile t lies on base face t * 12 // 8; all tiles of one face share one code.
All inputs are finite; a program needn't handle non-finite values.
Results may differ from the reference program's by a relative error of at most 0.022.
Values may be sent and summed in bfloat16 or wider, within the bound.
A program may use at most 64 MiB of HBM per device.

```python
import math
import jax
import jax.numpy as jnp
from jax import lax

CH = 64
HID = 256
TP = 16
MICRO = 4
LAYERS = 8
TILES = 8
GRID_COLS = 4
N_SECTION = 4


def tile_layout(key):
    face_key = jax.random.fold_in(key, 11)
    flag_key = jax.random.fold_in(key, 23)
    tile_ids = jnp.arange(TILES, dtype=jnp.int32)
    face_ids = tile_ids * 12 // TILES
    face_codes = jax.random.permutation(face_key, jnp.arange(12, dtype=jnp.int32) % 4)
    tile_codes = face_codes[face_ids]
    vertex_flags = jax.random.randint(flag_key, (TILES,), 0, 4, dtype=jnp.int32) == 0
    vertex_flags = vertex_flags.at[0].set(True)
    offsets = jnp.array([-GRID_COLS, 1, GRID_COLS, -1, 1 - GRID_COLS, GRID_COLS + 1, GRID_COLS - 1, -GRID_COLS - 1], dtype=jnp.int32)
    direction_ids = jnp.arange(8, dtype=jnp.int32)
    true_dirs = (direction_ids[None, :] % 4 + tile_codes[:, None]) % 4 + 4 * (direction_ids[None, :] // 4)
    targets = (tile_ids[:, None] + offsets[true_dirs]) % TILES
    south_west = vertex_flags[(tile_ids + GRID_COLS - 1) % TILES]
    missing = (true_dirs == 4) & vertex_flags[:, None] | (true_dirs == 6) & south_west[:, None]
    return (jnp.where(missing, -1, targets).astype(jnp.int32), tile_codes.astype(jnp.int32))


def draw_neighbours(key, part):
    return tile_layout(key)[0]


def draw_orientation(key, part):
    return tile_layout(key)[1]


def draw_inputs(key, part):
    noise_key = jax.random.fold_in(key, 3)
    channel_key = jax.random.fold_in(key, 5)
    pixel_key = jax.random.fold_in(key, 7)
    full_shape = (MICRO, TILES, TP, TP, CH)
    values = jnp.clip(jax.random.normal(noise_key, full_shape, jnp.float32), -4.0, 4.0)
    channel_scale = jnp.exp(jax.random.uniform(channel_key, (CH,), jnp.float32, -1.15, 1.15))
    pixel_scale = jnp.exp(jax.random.uniform(pixel_key, (MICRO, TILES, TP, TP, 1), jnp.float32, -1.15, 1.15))
    scaled = values * channel_scale * pixel_scale
    return scaled.reshape(MICRO, TILES, TP, TP * CH).astype(jnp.bfloat16)


def steps_of(rng, shape, cuts, smallest, largest):
    loudness, own = 1.0, jax.random.fold_in(rng, 6)
    for position, shards_of in cuts:
        heights = jnp.exp(jax.random.uniform(jax.random.fold_in(own, position), (shards_of,), jnp.float32, smallest / len(cuts), largest / len(cuts)))
        loudness = loudness * jnp.repeat(heights, shape[position] // shards_of).reshape([-1 if axis == position else 1 for axis in range(len(shape))])
    return loudness


def normal_values(own_key, shape, width, limit, shards=(), held_as=jnp.bfloat16):
    entries = width * jax.random.normal(own_key, shape, jnp.float32)
    if shards:
        entries = entries * steps_of(own_key, shape, shards, -0.22, 0.18)
    return jnp.clip(entries, -limit, limit).astype(held_as)


def setup_inputs(seed: int = 0) -> dict:
    key_list = jax.random.split(jax.random.key(seed), 8)
    inputs = draw_inputs(jax.random.fold_in(key_list[7], 71), 0)
    cotangent = normal_values(key_list[1], (MICRO, TILES, TP, TP * CH), 1.0, 6.0, ((1, 8),))
    depth_weight = normal_values(key_list[2], (LAYERS, 49, CH), 49 ** -0.5, 0.875, ((0, 4),))
    in_weight = normal_values(key_list[3], (LAYERS, CH, HID), CH ** -0.5, 0.75, ((0, 4),))
    out_weight = normal_values(key_list[4], (LAYERS, HID, CH), HID ** -0.5, 0.375, ((0, 4),))
    neighbours = draw_neighbours(jax.random.fold_in(key_list[7], 71), 0)
    orientation = draw_orientation(jax.random.fold_in(key_list[7], 71), 0)
    return dict(inputs=inputs, cotangent=cotangent, depth_weight=depth_weight, in_weight=in_weight, out_weight=out_weight, neighbours=neighbours, orientation=orientation)


norm_eps = 1e-06
rim_width = 3
kernel_side = 7

def layer_norm(values):
    centred = values - lax.optimization_barrier(jnp.mean(values, axis=-1, keepdims=True))
    spread = lax.optimization_barrier(jnp.mean(centred * centred, axis=-1, keepdims=True))
    return centred * lax.rsqrt(spread + norm_eps)

def smooth_gate(values):
    return jax.nn.gelu(values, approximate=True)

def depthwise(padded, depth_taps):
    extent = padded.shape[-2] - 2 * rim_width
    accum_total = jnp.zeros(padded.shape[:-3] + (extent, extent, padded.shape[-1]), jnp.float32)
    for tap_row in range(kernel_side):
        for tap_col in range(kernel_side):
            window = padded[..., tap_row:tap_row + extent, tap_col:tap_col + extent, :].astype(jnp.float32)
            accum_total = accum_total + window * depth_taps[tap_row * kernel_side + tap_col].astype(jnp.float32)
    return accum_total

def depthwise_back(padded, depth_taps, grad_hidden):
    extent = grad_hidden.shape[-2]
    leading = tuple(range(grad_hidden.ndim - 1))
    grad_pad = jnp.zeros(padded.shape, jnp.float32)
    tap_list = []
    for tap_row in range(kernel_side):
        for tap_col in range(kernel_side):
            window = padded[..., tap_row:tap_row + extent, tap_col:tap_col + extent, :].astype(jnp.float32)
            tap_list.append(lax.optimization_barrier(jnp.sum(grad_hidden * window, axis=leading)))
            weight_tap = depth_taps[tap_row * kernel_side + tap_col].astype(jnp.float32)
            grad_pad = grad_pad.at[..., tap_row:tap_row + extent, tap_col:tap_col + extent, :].add(grad_hidden * weight_tap)
    return (jnp.stack(tap_list), grad_pad)

def block_forward(padded, depth_taps, weight_in, weight_out):
    channels = padded.shape[-1]
    hidden = depthwise(padded, depth_taps)
    normed = layer_norm(hidden).astype(jnp.bfloat16)
    flat_rows = normed.reshape(-1, channels)
    gated = smooth_gate(jnp.dot(flat_rows, weight_in, preferred_element_type=jnp.float32)).astype(jnp.bfloat16)
    branch = jnp.dot(gated, weight_out, preferred_element_type=jnp.float32).reshape(hidden.shape)
    centre = padded[..., rim_width:-rim_width, rim_width:-rim_width, :].astype(jnp.float32)
    return (centre + branch).astype(jnp.bfloat16)

def block_backward(padded, depth_taps, weight_in, weight_out, upstream):
    channels = padded.shape[-1]
    hidden = depthwise(padded, depth_taps)
    normed = layer_norm(hidden).astype(jnp.bfloat16)
    flat_rows = normed.reshape(-1, channels)
    before = jnp.dot(flat_rows, weight_in, preferred_element_type=jnp.float32)
    gated = smooth_gate(before).astype(jnp.bfloat16)
    flow_rows = upstream.reshape(-1, channels)
    grad_out = jnp.dot(gated.T, flow_rows, preferred_element_type=jnp.float32)
    grad_gated = jnp.dot(flow_rows, weight_out.T, preferred_element_type=jnp.float32)
    grad_before = jax.vjp(smooth_gate, before)[1](grad_gated)[0].astype(jnp.bfloat16)
    grad_in = jnp.dot(flat_rows.T, grad_before, preferred_element_type=jnp.float32)
    grad_normed = jnp.dot(grad_before, weight_in.T, preferred_element_type=jnp.float32).reshape(hidden.shape)
    grad_hidden = jax.vjp(layer_norm, hidden)[1](grad_normed)[0]
    grad_depth, grad_pad = depthwise_back(padded, depth_taps, grad_hidden)
    return (grad_depth, grad_in, grad_out, grad_pad)

def offers(square):
    turned = [jnp.rot90(square, quarter, axes=(-3, -2)) for quarter in range(4)]
    strips = jnp.stack([rotated[..., -rim_width:, :, :] for rotated in turned], axis=-4)
    corners = jnp.stack([rotated[..., -rim_width:, :rim_width, :] for rotated in turned], axis=-4)
    return (strips, corners)

def assemble(square, rim_list):
    north, east, south, west, north_east, south_east, south_west, north_west = rim_list
    top_band = jnp.concatenate([north_west, north, north_east], axis=-2)
    middle_band = jnp.concatenate([west, square, east], axis=-2)
    bottom_band = jnp.concatenate([south_west, south, south_east], axis=-2)
    return jnp.concatenate([top_band, middle_band, bottom_band], axis=-3)

def rim_parts(grad_pad):
    extent = grad_pad.shape[-2] - 2 * rim_width
    edge_end = extent + rim_width
    return [grad_pad[..., :rim_width, rim_width:edge_end, :], grad_pad[..., rim_width:edge_end, edge_end:, :], grad_pad[..., edge_end:, rim_width:edge_end, :], grad_pad[..., rim_width:edge_end, :rim_width, :], grad_pad[..., :rim_width, edge_end:, :], grad_pad[..., edge_end:, edge_end:, :], grad_pad[..., edge_end:, :rim_width, :], grad_pad[..., :rim_width, :rim_width, :]]

def pad_tiles(values, neighbours, orientation):
    strips, corners = offers(values)
    rim_list = []
    for direction in range(8):
        turn_count = direction % 4
        target = neighbours[:, direction]
        safe_target = jnp.maximum(target, 0)
        quarter = ((turn_count + orientation) % 4 - orientation[safe_target]) % 4
        source = strips if direction < 4 else corners
        segment = jnp.rot90(source[safe_target, quarter], -turn_count, axes=(1, 2))
        keep_mask = (target >= 0)[:, None, None, None]
        rim_list.append(jnp.where(keep_mask, segment, jnp.zeros_like(segment)))
    return assemble(values, rim_list)

def unpad_tiles(grad_pad, neighbours, orientation):
    pieces = rim_parts(grad_pad)
    tile_count = grad_pad.shape[0]
    extent = grad_pad.shape[1] - 2 * rim_width
    channels = grad_pad.shape[-1]
    accum_total = jnp.zeros((tile_count, extent, extent, channels), grad_pad.dtype)
    for direction in range(8):
        turn_count = direction % 4
        target = neighbours[:, direction]
        safe_target = jnp.maximum(target, 0)
        quarter = ((turn_count + orientation) % 4 - orientation[safe_target]) % 4
        keep_mask = (target >= 0)[:, None, None, None]
        segment = jnp.rot90(pieces[direction], turn_count, axes=(1, 2))
        segment = jnp.where(keep_mask, segment, jnp.zeros_like(segment))
        canvas = jnp.zeros((tile_count, extent, extent, channels), grad_pad.dtype)
        if direction < 4:
            canvas = canvas.at[:, extent - rim_width:, :, :].set(segment)
        else:
            canvas = canvas.at[:, extent - rim_width:, :rim_width, :].set(segment)
        placed = jnp.zeros_like(canvas)
        for turns_back in range(4):
            chosen = (quarter == turns_back)[:, None, None, None]
            placed = placed + jnp.where(chosen, jnp.rot90(canvas, -turns_back, axes=(1, 2)), jnp.zeros_like(canvas))
        accum_total = accum_total.at[safe_target].add(placed)
    return accum_total

def reference(inputs, cotangent, depth_weight, in_weight, out_weight, neighbours, orientation):
    micro_count, tile_count, extent, merged = inputs.shape
    channels = depth_weight.shape[-1]
    layer_count = depth_weight.shape[0]
    per_section = layer_count // N_SECTION
    grad_scale = 1.0 / math.sqrt(micro_count * tile_count * extent * extent)

    def forward_layer(values, weights):
        depth_taps, weight_in, weight_out = weights
        padded = pad_tiles(values, neighbours, orientation)
        result = block_forward(padded, depth_taps, weight_in, weight_out)
        return (result, (padded, result))

    def backward_layer(upstream, items):
        depth_taps, weight_in, weight_out, padded = items
        grad_depth, grad_in, grad_out, grad_pad = block_backward(padded, depth_taps, weight_in, weight_out, upstream)
        interior = grad_pad[:, rim_width:-rim_width, rim_width:-rim_width, :]
        returned = unpad_tiles(grad_pad, neighbours, orientation)
        result = (upstream.astype(jnp.float32) + interior + returned).astype(jnp.bfloat16)
        return (result, (grad_depth, grad_in, grad_out, result))

    def one_micro(totals, micro_pair):
        begin_field, upstream = micro_pair
        values = begin_field.reshape(tile_count, extent, extent, channels)
        _, (pad_list, results) = lax.scan(forward_layer, values, (depth_weight, in_weight, out_weight))
        flow_start = upstream.reshape(tile_count, extent, extent, channels)
        _, (grad_depth, grad_in, grad_out, flows) = lax.scan(backward_layer, flow_start, (depth_weight, in_weight, out_weight, pad_list), reverse=True)
        totals = (totals[0] + grad_depth, totals[1] + grad_in, totals[2] + grad_out)
        out_list = results[per_section - 1::per_section].reshape(N_SECTION, tile_count, extent, merged)
        grad_list = flows[::per_section].reshape(N_SECTION, tile_count, extent, merged)
        return (totals, (out_list, grad_list))
    start_sums = (jnp.zeros(depth_weight.shape, jnp.float32), jnp.zeros(in_weight.shape, jnp.float32), jnp.zeros(out_weight.shape, jnp.float32))
    totals, (out_list, grad_list) = lax.scan(one_micro, start_sums, (inputs, cotangent))
    section_outputs = jnp.transpose(out_list, (1, 0, 2, 3, 4))
    section_grads = jnp.transpose(grad_list, (1, 0, 2, 3, 4))
    return (section_outputs, section_grads, totals[0] * grad_scale, totals[1] * grad_scale, totals[2] * grad_scale)
```

```python
import functools
import math

import jax
import jax.numpy as jnp
from jax import lax
from jax.experimental import pallas as pl
from jax.experimental.pallas import tpu as pltpu
from jax.sharding import PartitionSpec as P

norm_eps = 1e-06
rim = 3
side = 7
gelu_k = math.sqrt(2.0 / math.pi)
gelu_c = 0.044715
f32, bf16 = jnp.float32, jnp.bfloat16
WEST, EAST = 0, 1


def grid_offsets(tile_count):
    columns = max(tile_count // 8, 4)
    return [-columns, 1, columns, -1, 1 - columns, columns + 1, columns - 1, -columns - 1]


def unpacked(v):
    half = v.shape[1] // 2
    return jnp.concatenate([v[:, :half], v[:, half:]], axis=0)


def packed(v):
    half = v.shape[0] // 2
    return jnp.concatenate([v[:half], v[half:]], axis=1)


def mm(a, b, dims):
    return lax.dot_general(a, b, ((dims[0], dims[1]), ((), ())), preferred_element_type=f32)


def half_mean(v, averaging):
    high = v.astype(bf16)
    low = (v - high.astype(f32)).astype(bf16)
    return mm(jnp.concatenate([high, low], axis=1), averaging, ((1,), (0,)))


def kernel(
    tile_count,
    layers,
    x_ref,
    ct_ref,
    taps_ref,
    w1_ref,
    w2_ref,
    mask_ref,
    zo_ref,
    go_ref,
    dk_ref,
    dw1_ref,
    dw2_ref,
    pad,
    odd,
    es,
    fr,
    xhat,
    inv,
    us,
    gs,
    slope,
    dz,
    dodd,
    dp,
    eb,
    br,
    bn,
    field,
    grad,
    averaging,
    send_sem,
    frecv,
    brecv,
):
    me = lax.axis_index("tile")
    offsets = grid_offsets(tile_count)
    north, east, south, west, ne, se, sw, nw = [
        lax.rem(me + (off % tile_count), tile_count) for off in offsets
    ]

    def copies(plan, recv):
        return [
            pltpu.make_async_remote_copy(
                src_ref=src,
                dst_ref=dst,
                send_sem=send_sem.at[i],
                recv_sem=recv.at[i],
                device_id={"tile": target},
                device_id_type=pl.DeviceIdType.MESH,
            )
            for i, (target, src, dst) in enumerate(plan)
        ]

    def forward_copies(l):
        return copies(
            [
                (north, pad.at[l, 3:6, 8:16], pad.at[l, 19:22, 8:16]),
                (south, pad.at[l, 16:19, 8:16], pad.at[l, 0:3, 8:16]),
                (nw, es.at[WEST, :, 0:8], fr.at[l, EAST, :, 24:32]),
                (ne, es.at[EAST, :, 0:8], fr.at[l, WEST, :, 24:32]),
                (se, es.at[EAST, :, 8:16], fr.at[l, WEST, :, 0:8]),
                (sw, es.at[WEST, :, 8:16], fr.at[l, EAST, :, 0:8]),
                (east, es.at[EAST], fr.at[l, WEST, :, 8:24]),
                (west, es.at[WEST], fr.at[l, EAST, :, 8:24]),
            ],
            frecv.at[l],
        )

    def backward_copies(l):
        return copies(
            [
                (north, dp.at[0:3, 8:16], bn.at[l, 1]),
                (south, dp.at[19:22, 8:16], bn.at[l, 0]),
                (nw, eb.at[WEST, :, 0:8], br.at[l, EAST, :, 24:32]),
                (ne, eb.at[EAST, :, 0:8], br.at[l, WEST, :, 24:32]),
                (se, eb.at[EAST, :, 24:32], br.at[l, WEST, :, 16:24]),
                (sw, eb.at[WEST, :, 24:32], br.at[l, EAST, :, 16:24]),
                (east, eb.at[EAST, :, 8:24], br.at[l, WEST, :, 0:16]),
                (west, eb.at[WEST, :, 8:24], br.at[l, EAST, :, 0:16]),
            ],
            brecv.at[l],
        )

    def offer(l, z):
        pad[l, 3:19, 8:16, :] = z.reshape(16, 8, 128)
        field[...] = z
        for pair in range(2):
            es[WEST, pair] = field[pl.ds(pair, 16, stride=8), :]
            es[EAST, pair] = field[pl.ds(6 + pair, 16, stride=8), :]

    barrier = pltpu.get_barrier_semaphore()
    partners = sorted({off % tile_count for off in offsets})
    for off in partners:
        pl.semaphore_signal(
            barrier,
            inc=1,
            device_id={"tile": lax.rem(me + off, tile_count)},
            device_id_type=pl.DeviceIdType.MESH,
        )

    offer(0, x_ref[...])
    rows = lax.broadcasted_iota(jnp.int32, (256, 128), 0)
    lanes = lax.broadcasted_iota(jnp.int32, (256, 128), 1)
    same = ((rows % 128) < 64) == (lanes < 64)
    averaging[...] = jnp.where(same, 1.0 / 64.0, 0.0).astype(bf16)
    dz[...] = jnp.zeros_like(dz)
    dodd[...] = jnp.zeros_like(dodd)
    eb[...] = jnp.zeros_like(eb)
    pl.semaphore_wait(barrier, len(partners))
    for copy in forward_copies(0):
        copy.start()

    def low_lanes(shape):
        return lax.broadcasted_iota(jnp.int32, shape, len(shape) - 1) < 64

    def forward_step(l, carry):
        sent = forward_copies(l)
        for copy in sent:
            copy.wait_recv()
        for edge in range(2):
            for pair in range(2):
                column = fr[l, edge, pair, 5:27, :] * mask_ref[edge]
                place = (6 if edge == WEST else 16) + pair
                pad[l, :, place : place + 1, :] = column.reshape(22, 1, 128)
        keep = low_lanes((22, 16, 128))
        merged = jnp.where(keep, pad[l, :, 7:23, :], pad[l, :, 6:22, :])
        odd[l] = pltpu.roll(merged.reshape(22 * 16, 128), 64, 1).reshape(22, 16, 128)
        total = jnp.zeros((16, 8, 128), f32)
        for a in range(side):
            for b in range(side):
                if b % 2:
                    start = 6 + (b + 1) // 2
                    window = pad[l, a : a + 16, start : start + 8, :]
                else:
                    window = odd[l, a : a + 16, b // 2 : b // 2 + 8, :]
                total = total + window * taps_ref[l, side * a + b]
        h = total.reshape(128, 128)
        avg = averaging[...]
        centred = h - half_mean(h, avg)
        scale = lax.rsqrt(half_mean(centred * centred, avg) + norm_eps)
        normed = centred * scale
        xhat[l] = normed
        inv[l] = scale
        u = unpacked(normed.astype(bf16))
        us[l] = u
        before = mm(u, w1_ref[l], ((1,), (0,)))
        t = jnp.tanh(gelu_k * (before + gelu_c * before * before * before))
        g = (0.5 * before * (1.0 + t)).astype(bf16)
        gs[l] = g
        branch = packed(mm(g, w2_ref[l], ((1,), (0,))))
        z = pad[l, 3:19, 8:16, :].reshape(128, 128) + branch
        z16 = z.astype(bf16)
        zo_ref[l // 2] = z16
        for copy in sent:
            copy.wait_send()

        @pl.when(l < layers - 1)
        def _():
            offer(l + 1, z16.astype(f32))
            for copy in forward_copies(l + 1):
                copy.start()

        square = before * before
        slope[l] = 0.5 * (1.0 + t) + 0.5 * before * (1.0 - t * t) * gelu_k * (
            1.0 + 3.0 * gelu_c * square
        )
        return carry

    lax.fori_loop(0, layers, forward_step, 0)

    grad[...] = ct_ref[...]

    def backward_step(count, carry):
        l = layers - 1 - count
        d = grad[...]
        d_rows = unpacked(d.astype(bf16))
        dg = mm(d_rows, w2_ref[l], ((1,), (1,)))
        da = (dg * slope[l]).astype(bf16)
        du = packed(mm(da, w1_ref[l], ((1,), (1,))))
        avg = averaging[...]
        normed = xhat[l]
        dh = inv[l] * (du - half_mean(du, avg) - normed * half_mean(du * normed, avg))
        dh3 = dh.reshape(16, 8, 128)
        dz[6:22, 8:16, :] = dh3
        keep = low_lanes((16, 8, 128))
        for start in (0, 8):
            merged = jnp.where(
                keep, dz[6:22, start + 1 : start + 9, :], dz[6:22, start : start + 8, :]
            )
            rolled = pltpu.roll(merged.reshape(128, 128), 64, 1).reshape(16, 8, 128)
            dodd[6:22, start : start + 8, :] = rolled
        for top in (0, 11):
            total = jnp.zeros((11, 16, 128), f32)
            for a in range(side):
                for b in range(side):
                    shift = 3 - b
                    first = top + 6 - a
                    if shift % 2 == 0:
                        start = 6 + shift // 2
                        window = dz[first : first + 11, start : start + 16, :]
                    else:
                        start = 6 + (shift - 1) // 2
                        window = dodd[first : first + 11, start : start + 16, :]
                    total = total + window * taps_ref[l, side * a + b]
            dp[top : top + 11, 6:22, :] = total
        for edge in range(2):
            for pair in range(2):
                place = (6 if edge == WEST else 16) + pair
                column = dp[:, place : place + 1, :].reshape(22, 128)
                eb[edge, pair, 5:27, :] = column * mask_ref[edge]
        sent = backward_copies(l)
        for copy in sent:
            copy.start()

        for a in range(side):
            for b in range(side):
                if b % 2:
                    start = 6 + (b + 1) // 2
                    window = pad[l, a : a + 16, start : start + 8, :]
                else:
                    window = odd[l, a : a + 16, b // 2 : b // 2 + 8, :]
                part = jnp.sum(window * dh3, axis=0)
                dk_ref[l, side * a + b : side * a + b + 1, :] = jnp.sum(
                    part, axis=0, keepdims=True
                )
        dw1_ref[l] = mm(us[l], da, ((0,), (0,)))
        dw2_ref[l] = mm(gs[l], d_rows, ((0,), (0,)))

        for copy in sent:
            copy.wait_recv()
        base = d.reshape(16, 8, 128) + dp[3:19, 8:16, :]
        top_part = base[0:3] + bn[l, 0]
        bottom_part = base[13:16] + bn[l, 1]
        field[...] = jnp.concatenate([top_part, base[3:13], bottom_part], axis=0).reshape(128, 128)
        for edge in range(2):
            for pair in range(2):
                place = (0 if edge == WEST else 6) + pair
                extra = br[l, edge, pair, 0:16, :] + br[l, edge, pair, 16:32, :]
                field[pl.ds(place, 16, stride=8), :] = (
                    field[pl.ds(place, 16, stride=8), :] + extra
                )
        result = field[...].astype(bf16)
        go_ref[l // 2] = result
        grad[...] = result.astype(f32)
        for copy in sent:
            copy.wait_send()
        return carry

    lax.fori_loop(0, layers, backward_step, 0)


def turned(n, code):
    cells = jnp.arange(n * n, dtype=jnp.int32)
    r, c = cells // n, cells % n
    choices = [r * n + c, c * n + (n - 1 - r), (n - 1 - r) * n + (n - 1 - c), (n - 1 - c) * n + r]
    source = choices[0]
    for k in range(1, 4):
        source = jnp.where(code == k, choices[k], source)
    return (source[:, None] == cells[None, :])


def on_device(inputs, cotangent, depth_weight, in_weight, out_weight, neighbours, orientation):
    micro_count, _, extent, merged = inputs.shape
    blocks, taps, channels = depth_weight.shape
    hidden = in_weight.shape[2]
    tile_count = lax.axis_size("tile")
    sections = lax.axis_size("section")
    layers = blocks * sections
    section_id = lax.axis_index("section")
    code = orientation[lax.axis_index("tile")]
    back_code = (-code) % 4
    grad_scale = 1.0 / math.sqrt(micro_count * tile_count * extent * extent)
    pixels = extent * extent

    mine = jnp.stack([inputs[:, 0], cotangent[:, 0]])
    mine = lax.dynamic_index_in_dim(mine, section_id, 1, keepdims=False)
    into = turned(extent, back_code).astype(bf16)
    mine = jnp.einsum(
        "pq,fqc->fpc", into, mine.reshape(2, pixels, channels), preferred_element_type=f32
    )
    mine = mine.reshape(2, pixels // 2, 2 * channels)

    depth_all = lax.all_gather(depth_weight, "section", axis=0, tiled=True)
    in_all = lax.all_gather(in_weight, "section", axis=0, tiled=True)
    out_all = lax.all_gather(out_weight, "section", axis=0, tiled=True)
    taps_turn = turned(side, back_code)
    taps_all = jnp.einsum(
        "pq,lqc->lpc", taps_turn.astype(bf16), depth_all, preferred_element_type=f32
    )
    taps_all = jnp.concatenate([taps_all, taps_all], axis=2)

    ne_ok = (neighbours[0, 4 + back_code] >= 0).astype(f32)
    sw_ok = (neighbours[0, 4 + (2 - code) % 4] >= 0).astype(f32)
    rows = jnp.arange(extent + 2 * rim)
    mask = jnp.stack([jnp.where(rows >= 19, sw_ok, 1.0), jnp.where(rows < 3, ne_ok, 1.0)])
    mask = jnp.broadcast_to(mask[:, :, None], (2, extent + 2 * rim, 128))

    vmem = pl.BlockSpec(memory_space=pltpu.VMEM)
    zo, go, dk, dw1, dw2 = pl.pallas_call(
        functools.partial(kernel, tile_count, layers),
        out_shape=(
            jax.ShapeDtypeStruct((sections, 128, 128), bf16),
            jax.ShapeDtypeStruct((sections, 128, 128), bf16),
            jax.ShapeDtypeStruct((layers, taps, 128), f32),
            jax.ShapeDtypeStruct((layers, channels, hidden), f32),
            jax.ShapeDtypeStruct((layers, hidden, channels), f32),
        ),
        in_specs=[vmem] * 6,
        out_specs=(vmem,) * 5,
        scratch_shapes=[
            pltpu.VMEM((layers, 22, 24, 128), f32),
            pltpu.VMEM((layers, 22, 16, 128), f32),
            pltpu.VMEM((2, 2, 16, 128), f32),
            pltpu.VMEM((layers, 2, 2, 32, 128), f32),
            pltpu.VMEM((layers, 128, 128), f32),
            pltpu.VMEM((layers, 128, 128), f32),
            pltpu.VMEM((layers, 256, 64), bf16),
            pltpu.VMEM((layers, 256, 256), bf16),
            pltpu.VMEM((layers, 256, 256), f32),
            pltpu.VMEM((28, 24, 128), f32),
            pltpu.VMEM((28, 24, 128), f32),
            pltpu.VMEM((22, 24, 128), f32),
            pltpu.VMEM((2, 2, 32, 128), f32),
            pltpu.VMEM((layers, 2, 2, 32, 128), f32),
            pltpu.VMEM((layers, 2, 3, 8, 128), f32),
            pltpu.VMEM((128, 128), f32),
            pltpu.VMEM((128, 128), f32),
            pltpu.VMEM((256, 128), bf16),
            pltpu.SemaphoreType.DMA((8,)),
            pltpu.SemaphoreType.DMA((layers, 8)),
            pltpu.SemaphoreType.DMA((layers, 8)),
        ],
        compiler_params=pltpu.CompilerParams(
            collective_id=0, has_side_effects=True, vmem_limit_bytes=40 * 1024 * 1024
        ),
    )(mine[0], mine[1], taps_all, in_all, out_all, mask)

    fields = jnp.stack([zo, go], axis=1).reshape(sections, 2, pixels, channels)
    outward = turned(extent, code).astype(bf16)
    fields = jnp.einsum("pq,sfqc->sfpc", outward, fields, preferred_element_type=f32).astype(bf16)
    fields = lax.all_to_all(fields, "section", 0, 0, tiled=True)
    section_outputs = fields[:, 0].reshape(1, micro_count, 1, extent, merged)
    section_grads = fields[:, 1].reshape(1, micro_count, 1, extent, merged)

    dk = dk[:, :, :channels] + dk[:, :, channels:]
    dk = jnp.einsum(
        "pq,lqc->lpc",
        turned(side, code).astype(f32),
        dk,
        precision=lax.Precision.HIGHEST,
        preferred_element_type=f32,
    )
    sums = jnp.concatenate(
        [dk.reshape(layers, -1), dw1.reshape(layers, -1), dw2.reshape(layers, -1)], axis=1
    )
    sums = lax.psum_scatter(sums, "section", scatter_dimension=0, tiled=True)
    sums = lax.psum(sums, "tile") * grad_scale
    cut1 = taps * channels
    cut2 = cut1 + channels * hidden
    return (
        section_outputs,
        section_grads,
        sums[:, :cut1].reshape(blocks, taps, channels),
        sums[:, cut1:cut2].reshape(blocks, channels, hidden),
        sums[:, cut2:].reshape(blocks, hidden, channels),
    )


def solution(mesh):
    in_specs = (
        P(None, "tile", None, None),
        P(None, "tile", None, None),
        P("section", None, None),
        P("section", None, None),
        P("section", None, None),
        P("tile", None),
        P(),
    )
    out_specs = (
        P("section", None, "tile", None, None),
        P("section", None, "tile", None, None),
        P("section", None, None),
        P("section", None, None),
        P("section", None, None),
    )
    return jax.shard_map(
        on_device, mesh=mesh, in_specs=in_specs, out_specs=out_specs, check_vma=False
    )
```

```python
import functools
import math

import jax
import jax.numpy as jnp
from jax import lax
from jax.experimental import pallas as pl
from jax.experimental.pallas import tpu as pltpu
from jax.sharding import PartitionSpec as P

norm_eps = 1e-06
rim = 3
side = 7
gelu_k = math.sqrt(2.0 / math.pi)
gelu_c = 0.044715
f32, bf16 = jnp.float32, jnp.bfloat16
WEST, EAST = 0, 1


def grid_offsets(tile_count):
    columns = max(tile_count // 8, 4)
    return [-columns, 1, columns, -1, 1 - columns, columns + 1, columns - 1, -columns - 1]


def unpacked(v):
    half = v.shape[1] // 2
    return jnp.concatenate([v[:, :half], v[:, half:]], axis=0)


def packed(v):
    half = v.shape[0] // 2
    return jnp.concatenate([v[:half], v[half:]], axis=1)


def mm(a, b, dims):
    return lax.dot_general(a, b, ((dims[0], dims[1]), ((), ())), preferred_element_type=f32)


def half_mean(v, averaging):
    high = v.astype(bf16)
    low = (v - high.astype(f32)).astype(bf16)
    return mm(jnp.concatenate([high, low], axis=1), averaging, ((1,), (0,)))


def kernel(
    tile_count,
    sections,
    blocks,
    piece,
    grad_scale,
    x_ref,
    ct_ref,
    taps_own,
    w1_own,
    w2_own,
    mask_ref,
    perm_ref,
    tap_perm_ref,
    zo_ref,
    go_ref,
    dk_out,
    dw1_out,
    dw2_out,
    taps_raw,
    taps_ref,
    w1_ref,
    w2_ref,
    zst,
    gst,
    zrec,
    grec,
    out_field,
    dk_ref,
    part,
    arec,
    total_ref,
    rs,
    fin,
    pad,
    odd,
    es,
    fr,
    xhat,
    inv,
    us,
    gs,
    slope,
    dz,
    dodd,
    dp,
    eb,
    br,
    bn,
    field,
    grad,
    averaging,
    send_sem,
    frecv,
    brecv,
    wsend,
    wrecv,
    zsend,
    zrecv,
    gsend,
    grecv,
    asend,
    arecv,
    rsend,
    rrecv,
    csend,
    crecv,
):
    layers = sections * blocks
    me = lax.axis_index("tile")
    mine = lax.axis_index("section")
    others = [lax.rem(mine + k, sections) for k in range(1, sections)]

    def across(axis, target, src, dst, send, recv):
        return pltpu.make_async_remote_copy(
            src_ref=src,
            dst_ref=dst,
            send_sem=send,
            recv_sem=recv,
            device_id={axis: target},
            device_id_type=pl.DeviceIdType.MESH,
        )

    def weight_copies(target, source):
        return [
            across("section", target, ref.at[source], ref.at[source], wsend.at[target, i], wrecv.at[source, i])
            for i, ref in enumerate((taps_raw, w1_ref, w2_ref))
        ]

    def z_copy(target, source):
        return across("section", target, zst.at[target], zrec.at[source], zsend.at[target], zrecv.at[source])

    def g_copy(target, source):
        return across("section", target, gst.at[target], grec.at[source], gsend.at[target], grecv.at[source])

    def part_copy(l, target, source):
        i = lax.rem(l, blocks)
        return across("section", target, part.at[l], arec.at[source, i], asend.at[l], arecv.at[source, i])

    def restored(v16):
        out_field[...] = packed(mm(perm_ref[...], unpacked(v16), ((0,), (0,))))
        columns = [out_field[pl.ds(k, 16, stride=8), :] for k in range(8)]
        return jnp.concatenate(columns, axis=1).astype(bf16)

    def taken(v):
        v = v.astype(f32)
        for k in range(8):
            out_field[pl.ds(k, 16, stride=8), :] = v[:, 128 * k : 128 * k + 128]
        rows16 = unpacked(out_field[...].astype(bf16))
        return packed(mm(perm_ref[...], rows16, ((1,), (0,))))

    offsets = grid_offsets(tile_count)
    north, east, south, west, ne, se, sw, nw = [
        lax.rem(me + (off % tile_count), tile_count) for off in offsets
    ]

    def copies(plan, recv):
        return [
            pltpu.make_async_remote_copy(
                src_ref=src,
                dst_ref=dst,
                send_sem=send_sem.at[i],
                recv_sem=recv.at[i],
                device_id={"tile": target},
                device_id_type=pl.DeviceIdType.MESH,
            )
            for i, (target, src, dst) in enumerate(plan)
        ]

    def forward_copies(l):
        return copies(
            [
                (north, pad.at[l, 3:6, 8:16], pad.at[l, 19:22, 8:16]),
                (south, pad.at[l, 16:19, 8:16], pad.at[l, 0:3, 8:16]),
                (nw, es.at[WEST, :, 0:8], fr.at[l, EAST, :, 24:32]),
                (ne, es.at[EAST, :, 0:8], fr.at[l, WEST, :, 24:32]),
                (se, es.at[EAST, :, 8:16], fr.at[l, WEST, :, 0:8]),
                (sw, es.at[WEST, :, 8:16], fr.at[l, EAST, :, 0:8]),
                (east, es.at[EAST], fr.at[l, WEST, :, 8:24]),
                (west, es.at[WEST], fr.at[l, EAST, :, 8:24]),
            ],
            frecv.at[l],
        )

    def backward_copies(l):
        return copies(
            [
                (north, dp.at[0:3, 8:16], bn.at[l, 1]),
                (south, dp.at[19:22, 8:16], bn.at[l, 0]),
                (nw, eb.at[WEST, :, 0:8], br.at[l, EAST, :, 24:32]),
                (ne, eb.at[EAST, :, 0:8], br.at[l, WEST, :, 24:32]),
                (se, eb.at[EAST, :, 24:32], br.at[l, WEST, :, 16:24]),
                (sw, eb.at[WEST, :, 24:32], br.at[l, EAST, :, 16:24]),
                (east, eb.at[EAST, :, 8:24], br.at[l, WEST, :, 0:16]),
                (west, eb.at[WEST, :, 8:24], br.at[l, EAST, :, 0:16]),
            ],
            brecv.at[l],
        )

    def offer(l, z):
        pad[l, 3:19, 8:16, :] = z.reshape(16, 8, 128)
        field[...] = z
        for pair in range(2):
            es[WEST, pair] = field[pl.ds(pair, 16, stride=8), :]
            es[EAST, pair] = field[pl.ds(6 + pair, 16, stride=8), :]

    barrier = pltpu.get_barrier_semaphore()

    def greet(j, carry):
        pl.semaphore_signal(
            barrier,
            inc=1,
            device_id={"tile": lax.rem(me + j, tile_count)},
            device_id_type=pl.DeviceIdType.MESH,
        )
        return carry

    lax.fori_loop(1, tile_count, greet, 0)
    for other in others:
        pl.semaphore_signal(
            barrier,
            inc=1,
            device_id={"section": other},
            device_id_type=pl.DeviceIdType.MESH,
        )
    taps_raw[mine] = taps_own[...]
    w1_ref[mine] = w1_own[...]
    w2_ref[mine] = w2_own[...]
    offer(0, taken(x_ref[mine]))
    rows = lax.broadcasted_iota(jnp.int32, (256, 128), 0)
    lanes = lax.broadcasted_iota(jnp.int32, (256, 128), 1)
    same = ((rows % 128) < 64) == (lanes < 64)
    averaging[...] = jnp.where(same, 1.0 / 64.0, 0.0).astype(bf16)
    dz[...] = jnp.zeros_like(dz)
    dodd[...] = jnp.zeros_like(dodd)
    eb[...] = jnp.zeros_like(eb)
    pl.semaphore_wait(barrier, tile_count - 1 + sections - 1)
    for copy in forward_copies(0):
        copy.start()
    for other in others:
        for copy in weight_copies(other, mine):
            copy.start()
    grad[...] = taken(ct_ref[mine])
    total_ref[...] = jnp.zeros_like(total_ref)
    dk_ref[...] = jnp.zeros_like(dk_ref)

    def low_lanes(shape):
        return lax.broadcasted_iota(jnp.int32, shape, len(shape) - 1) < 64

    def forward_step(l, carry):
        sec, block = l // blocks, lax.rem(l, blocks)

        @pl.when((block == 0) & (sec != mine))
        def _():
            for copy in weight_copies(mine, sec):
                copy.wait_recv()

        taps_ref[l] = mm(tap_perm_ref[...], taps_raw[sec, block], ((1,), (0,)))
        sent = forward_copies(l)
        for copy in sent:
            copy.wait_recv()
        for edge in range(2):
            for pair in range(2):
                column = fr[l, edge, pair, 5:27, :] * mask_ref[edge]
                place = (6 if edge == WEST else 16) + pair
                pad[l, :, place : place + 1, :] = column.reshape(22, 1, 128)
        keep = low_lanes((22, 16, 128))
        merged = jnp.where(keep, pad[l, :, 7:23, :], pad[l, :, 6:22, :])
        odd[l] = pltpu.roll(merged.reshape(22 * 16, 128), 64, 1).reshape(22, 16, 128)
        total = jnp.zeros((16, 8, 128), f32)
        for a in range(side):
            for b in range(side):
                if b % 2:
                    start = 6 + (b + 1) // 2
                    window = pad[l, a : a + 16, start : start + 8, :]
                else:
                    window = odd[l, a : a + 16, b // 2 : b // 2 + 8, :]
                total = total + window * taps_ref[l, side * a + b]
        h = total.reshape(128, 128)
        avg = averaging[...]
        centred = h - half_mean(h, avg)
        scale = lax.rsqrt(half_mean(centred * centred, avg) + norm_eps)
        normed = centred * scale
        xhat[l] = normed
        inv[l] = scale
        u = unpacked(normed.astype(bf16))
        us[l] = u
        before = mm(u, w1_ref[sec, block], ((1,), (0,)))
        t = jnp.tanh(gelu_k * (before + gelu_c * before * before * before))
        g = (0.5 * before * (1.0 + t)).astype(bf16)
        gs[l] = g
        branch = packed(mm(g, w2_ref[sec, block], ((1,), (0,))))
        z = pad[l, 3:19, 8:16, :].reshape(128, 128) + branch
        z16 = z.astype(bf16)
        for copy in sent:
            copy.wait_send()

        @pl.when(l < layers - 1)
        def _():
            offer(l + 1, z16.astype(f32))
            for copy in forward_copies(l + 1):
                copy.start()

        square = before * before
        @pl.when(block == blocks - 1)
        def _():
            zst[sec] = restored(z16)

        @pl.when((block == blocks - 1) & (sec != mine))
        def _():
            z_copy(sec, mine).start()

        slope[l] = 0.5 * (1.0 + t) + 0.5 * before * (1.0 - t * t) * gelu_k * (
            1.0 + 3.0 * gelu_c * square
        )
        return carry

    lax.fori_loop(0, layers, forward_step, 0)

    def backward_step(count, carry):
        l = layers - 1 - count
        sec, block = l // blocks, lax.rem(l, blocks)
        d = grad[...]
        d_rows = unpacked(d.astype(bf16))
        dg = mm(d_rows, w2_ref[sec, block], ((1,), (1,)))
        da = (dg * slope[l]).astype(bf16)
        du = packed(mm(da, w1_ref[sec, block], ((1,), (1,))))
        avg = averaging[...]
        normed = xhat[l]
        dh = inv[l] * (du - half_mean(du, avg) - normed * half_mean(du * normed, avg))
        dh3 = dh.reshape(16, 8, 128)
        dz[6:22, 8:16, :] = dh3
        keep = low_lanes((16, 8, 128))
        for start in (0, 8):
            merged = jnp.where(
                keep, dz[6:22, start + 1 : start + 9, :], dz[6:22, start : start + 8, :]
            )
            rolled = pltpu.roll(merged.reshape(128, 128), 64, 1).reshape(16, 8, 128)
            dodd[6:22, start : start + 8, :] = rolled
        for top in (0, 11):
            total = jnp.zeros((11, 16, 128), f32)
            for a in range(side):
                for b in range(side):
                    shift = 3 - b
                    first = top + 6 - a
                    if shift % 2 == 0:
                        start = 6 + shift // 2
                        window = dz[first : first + 11, start : start + 16, :]
                    else:
                        start = 6 + (shift - 1) // 2
                        window = dodd[first : first + 11, start : start + 16, :]
                    total = total + window * taps_ref[l, side * a + b]
            dp[top : top + 11, 6:22, :] = total
        for edge in range(2):
            for pair in range(2):
                place = (6 if edge == WEST else 16) + pair
                column = dp[:, place : place + 1, :].reshape(22, 128)
                eb[edge, pair, 5:27, :] = column * mask_ref[edge]
        sent = backward_copies(l)
        for copy in sent:
            copy.start()

        for a in range(side):
            for b in range(side):
                if b % 2:
                    start = 6 + (b + 1) // 2
                    window = pad[l, a : a + 16, start : start + 8, :]
                else:
                    window = odd[l, a : a + 16, b // 2 : b // 2 + 8, :]
                tap_rows = jnp.sum(window * dh3, axis=0)
                dk_ref[side * a + b : side * a + b + 1, :] = jnp.sum(
                    tap_rows, axis=0, keepdims=True
                )
        grad_in = mm(us[l], da, ((0,), (0,)))
        grad_out = mm(gs[l], d_rows, ((0,), (0,)))

        part[l, 0:128] = jnp.concatenate([grad_in[:, :128], grad_in[:, 128:]], axis=0).astype(bf16)
        part[l, 128:256] = packed(grad_out).astype(bf16)
        tap_sums = dk_ref[...]
        high = tap_sums.astype(bf16)
        low = (tap_sums - high.astype(f32)).astype(bf16)
        turn = tap_perm_ref[...]
        part[l, 256:320] = (mm(turn, high, ((0,), (0,))) + mm(turn, low, ((0,), (0,)))).astype(bf16)

        @pl.when(sec != mine)
        def _():
            part_copy(l, sec, mine).start()

        for copy in sent:
            copy.wait_recv()
        base = d.reshape(16, 8, 128) + dp[3:19, 8:16, :]
        top_part = base[0:3] + bn[l, 0]
        bottom_part = base[13:16] + bn[l, 1]
        field[...] = jnp.concatenate([top_part, base[3:13], bottom_part], axis=0).reshape(128, 128)
        for edge in range(2):
            for pair in range(2):
                place = (0 if edge == WEST else 6) + pair
                extra = br[l, edge, pair, 0:16, :] + br[l, edge, pair, 16:32, :]
                field[pl.ds(place, 16, stride=8), :] = (
                    field[pl.ds(place, 16, stride=8), :] + extra
                )
        result = field[...].astype(bf16)
        grad[...] = result.astype(f32)

        @pl.when(block == 0)
        def _():
            gst[sec] = restored(result)

        @pl.when((block == 0) & (sec != mine))
        def _():
            g_copy(sec, mine).start()

        for copy in sent:
            copy.wait_send()
        return carry

    lax.fori_loop(0, layers, backward_step, 0)

    for i in range(blocks):
        total = part[mine * blocks + i].astype(f32)
        for other in others:
            part_copy(mine * blocks + i, mine, other).wait_recv()
            total = total + arec[other, i].astype(f32)
        total_ref[320 * i : 320 * i + 320] = total.astype(bf16)

    def place(tile):
        return pl.ds(pl.multiple_of(tile * piece, 16), piece)

    def ahead(j):
        return lax.rem(me + j, tile_count)

    def behind(j):
        return lax.rem(me + tile_count - j, tile_count)

    def scatter(j, tile):
        return across("tile", tile, total_ref.at[place(tile)], rs.at[j], rsend.at[j], rrecv.at[j])

    def spread(j, tile, source):
        spot = place(source)
        return across("tile", tile, fin.at[spot], fin.at[spot], csend.at[j], crecv.at[j])

    def each(body):
        def step(j, carry):
            body(j)
            return carry

        lax.fori_loop(1, tile_count, step, 0)

    each(lambda j: scatter(j, ahead(j)).start())

    def gathered(j, total):
        scatter(j, ahead(j)).wait_recv()
        return total + rs[j].astype(f32)

    total = lax.fori_loop(1, tile_count, gathered, total_ref[place(me)].astype(f32))
    fin[place(me)] = (total * grad_scale).astype(bf16)
    each(lambda j: spread(j, ahead(j), me).start())

    zo_ref[mine] = zst[mine]
    go_ref[mine] = gst[mine]
    for other in others:
        z_copy(mine, other).wait_recv()
        zo_ref[other] = zrec[other]
        g_copy(mine, other).wait_recv()
        go_ref[other] = grec[other]
    for other in others:
        for copy in weight_copies(other, mine):
            copy.wait_send()
        z_copy(other, mine).wait_send()
        g_copy(other, mine).wait_send()
        for i in range(blocks):
            part_copy(other * blocks + i, other, mine).wait_send()
    each(lambda j: scatter(j, ahead(j)).wait_send())
    each(lambda j: spread(j, me, behind(j)).wait_recv())
    each(lambda j: spread(j, ahead(j), me).wait_send())
    for i in range(blocks):
        whole = fin[320 * i : 320 * i + 320].astype(f32)
        dw1_out[i] = jnp.concatenate([whole[0:64], whole[64:128]], axis=1)
        dw2_out[i] = unpacked(whole[128:256])
        dk_out[i] = whole[256:305, :64] + whole[256:305, 64:]


def turned(n, code, order):
    r, c = order // n, order % n
    choices = [r * n + c, c * n + (n - 1 - r), (n - 1 - r) * n + (n - 1 - c), (n - 1 - c) * n + r]
    source = choices[0]
    for k in range(1, 4):
        source = jnp.where(code == k, choices[k], source)
    return (source[:, None] == order[None, :]).astype(bf16)


def on_device(inputs, cotangent, depth_weight, in_weight, out_weight, neighbours, orientation):
    micro_count, _, extent, merged = inputs.shape
    blocks, taps, channels = depth_weight.shape
    hidden = in_weight.shape[2]
    tile_count = lax.axis_size("tile")
    sections = lax.axis_size("section")
    layers = blocks * sections
    code = orientation[lax.axis_index("tile")]
    back_code = (-code) % 4
    grad_scale = 1.0 / math.sqrt(micro_count * tile_count * extent * extent)
    pixels = extent * extent
    piece = -(-320 * blocks // (16 * tile_count)) * 16

    places = jnp.arange(pixels, dtype=jnp.int32)
    perm = turned(extent, back_code, (places % 128) * 2 + places // 128)
    tap_perm = turned(side, back_code, jnp.arange(taps, dtype=jnp.int32))
    tap_perm = jnp.pad(tap_perm, ((0, 64 - taps), (0, 64 - taps)))
    taps_own = jnp.concatenate([depth_weight, depth_weight], axis=2)
    taps_own = jnp.pad(taps_own, ((0, 0), (0, 64 - taps), (0, 0)))

    ne_ok = (neighbours[0, 4 + back_code] >= 0).astype(f32)
    sw_ok = (neighbours[0, 4 + (2 - code) % 4] >= 0).astype(f32)
    rows = jnp.arange(extent + 2 * rim)
    mask = jnp.stack([jnp.where(rows >= 19, sw_ok, 1.0), jnp.where(rows < 3, ne_ok, 1.0)])
    mask = jnp.broadcast_to(mask[:, :, None], (2, extent + 2 * rim, 128))

    vmem = pl.BlockSpec(memory_space=pltpu.VMEM)
    zo, go, dk, dw1, dw2 = pl.pallas_call(
        functools.partial(kernel, tile_count, sections, blocks, piece, grad_scale),
        out_shape=(
            jax.ShapeDtypeStruct((micro_count, extent, merged), bf16),
            jax.ShapeDtypeStruct((micro_count, extent, merged), bf16),
            jax.ShapeDtypeStruct((blocks, taps, channels), f32),
            jax.ShapeDtypeStruct((blocks, channels, hidden), f32),
            jax.ShapeDtypeStruct((blocks, hidden, channels), f32),
        ),
        in_specs=[vmem] * 8,
        out_specs=(vmem,) * 5,
        scratch_shapes=[
            pltpu.VMEM((sections, blocks, 64, 128), bf16),
            pltpu.VMEM((layers, 64, 128), f32),
            pltpu.VMEM((sections, blocks, channels, hidden), bf16),
            pltpu.VMEM((sections, blocks, hidden, channels), bf16),
            pltpu.VMEM((sections, 16, 1024), bf16),
            pltpu.VMEM((sections, 16, 1024), bf16),
            pltpu.VMEM((sections, 16, 1024), bf16),
            pltpu.VMEM((sections, 16, 1024), bf16),
            pltpu.VMEM((128, 128), f32),
            pltpu.VMEM((64, 128), f32),
            pltpu.VMEM((layers, 320, 128), bf16),
            pltpu.VMEM((sections, blocks, 320, 128), bf16),
            pltpu.VMEM((piece * tile_count, 128), bf16),
            pltpu.VMEM((tile_count, piece, 128), bf16),
            pltpu.VMEM((piece * tile_count, 128), bf16),
            pltpu.VMEM((layers, 22, 24, 128), f32),
            pltpu.VMEM((layers, 22, 16, 128), f32),
            pltpu.VMEM((2, 2, 16, 128), f32),
            pltpu.VMEM((layers, 2, 2, 32, 128), f32),
            pltpu.VMEM((layers, 128, 128), f32),
            pltpu.VMEM((layers, 128, 128), f32),
            pltpu.VMEM((layers, 256, 64), bf16),
            pltpu.VMEM((layers, 256, 256), bf16),
            pltpu.VMEM((layers, 256, 256), f32),
            pltpu.VMEM((28, 24, 128), f32),
            pltpu.VMEM((28, 24, 128), f32),
            pltpu.VMEM((22, 24, 128), f32),
            pltpu.VMEM((2, 2, 32, 128), f32),
            pltpu.VMEM((layers, 2, 2, 32, 128), f32),
            pltpu.VMEM((layers, 2, 3, 8, 128), f32),
            pltpu.VMEM((128, 128), f32),
            pltpu.VMEM((128, 128), f32),
            pltpu.VMEM((256, 128), bf16),
            pltpu.SemaphoreType.DMA((8,)),
            pltpu.SemaphoreType.DMA((layers, 8)),
            pltpu.SemaphoreType.DMA((layers, 8)),
            pltpu.SemaphoreType.DMA((sections, 3)),
            pltpu.SemaphoreType.DMA((sections, 3)),
            pltpu.SemaphoreType.DMA((sections,)),
            pltpu.SemaphoreType.DMA((sections,)),
            pltpu.SemaphoreType.DMA((sections,)),
            pltpu.SemaphoreType.DMA((sections,)),
            pltpu.SemaphoreType.DMA((layers,)),
            pltpu.SemaphoreType.DMA((sections, blocks)),
            pltpu.SemaphoreType.DMA((tile_count,)),
            pltpu.SemaphoreType.DMA((tile_count,)),
            pltpu.SemaphoreType.DMA((tile_count,)),
            pltpu.SemaphoreType.DMA((tile_count,)),
        ],
        compiler_params=pltpu.CompilerParams(
            collective_id=0, has_side_effects=True, vmem_limit_bytes=40 * 1024 * 1024
        ),
    )(
        inputs[:, 0],
        cotangent[:, 0],
        taps_own,
        in_weight,
        out_weight,
        mask,
        perm,
        tap_perm,
    )
    return (zo[None, :, None], go[None, :, None], dk, dw1, dw2)


def solution(mesh):
    in_specs = (
        P(None, "tile", None, None),
        P(None, "tile", None, None),
        P("section", None, None),
        P("section", None, None),
        P("section", None, None),
        P("tile", None),
        P(),
    )
    out_specs = (
        P("section", None, "tile", None, None),
        P("section", None, "tile", None, None),
        P("section", None, None),
        P("section", None, None),
        P("section", None, None),
    )
    return jax.shard_map(
        on_device, mesh=mesh, in_specs=in_specs, out_specs=out_specs, check_vma=False
    )
```

```python
import functools
import math

import jax
import jax.numpy as jnp
from jax import lax
from jax.experimental import pallas as pl
from jax.experimental.pallas import tpu as pltpu
from jax.sharding import PartitionSpec as P

norm_eps = 1e-06
rim = 3
side = 7
gelu_k = math.sqrt(2.0 / math.pi)
gelu_c = 0.044715
f32, bf16 = jnp.float32, jnp.bfloat16
WEST, EAST = 0, 1


def grid_offsets(tile_count):
    columns = max(tile_count // 8, 4)
    return [-columns, 1, columns, -1, 1 - columns, columns + 1, columns - 1, -columns - 1]


def unpacked(v):
    half = v.shape[1] // 2
    return jnp.concatenate([v[:, :half], v[:, half:]], axis=0)


def packed(v):
    half = v.shape[0] // 2
    return jnp.concatenate([v[:half], v[half:]], axis=1)


def mm(a, b, dims):
    return lax.dot_general(a, b, ((dims[0], dims[1]), ((), ())), preferred_element_type=f32)


def half_mean(v, averaging):
    high = v.astype(bf16)
    low = (v - high.astype(f32)).astype(bf16)
    return mm(jnp.concatenate([high, low], axis=1), averaging, ((1,), (0,)))


def turned(n, code, place, cell):
    r, c = place // n, place % n
    source = place
    for k, choice in ((1, c * n + n - 1 - r), (2, n * n - 1 - place), (3, (n - 1 - c) * n + r)):
        source = jnp.where(code == k, choice, source)
    return jnp.where(source == cell, 1.0, 0.0).astype(bf16)


def kernel(
    tile_count,
    sections,
    blocks,
    piece,
    grad_scale,
    x_ref,
    ct_ref,
    taps_own,
    w1_own,
    w2_own,
    neighbour_ref,
    orientation_ref,
    zo_ref,
    go_ref,
    dk_out,
    dw1_out,
    dw2_out,
    mask_ref,
    perm_ref,
    tap_perm_ref,
    rims,
    taps_raw,
    taps_ref,
    w1_ref,
    w2_ref,
    zst,
    gst,
    zrec,
    grec,
    out_field,
    dk_ref,
    part,
    arec,
    total_ref,
    rs,
    fin,
    pad,
    odd,
    es,
    fr,
    xhat,
    inv,
    us,
    gs,
    slope,
    dz,
    dodd,
    dp,
    eb,
    br,
    bn,
    field,
    grad,
    averaging,
    send_sem,
    frecv,
    brecv,
    wsend,
    wrecv,
    zsend,
    zrecv,
    gsend,
    grecv,
    asend,
    arecv,
    rsend,
    rrecv,
    csend,
    crecv,
):
    layers = sections * blocks
    me = lax.axis_index("tile")
    mine = lax.axis_index("section")
    others = [lax.rem(mine + k, sections) for k in range(1, sections)]

    def across(axis, target, src, dst, send, recv):
        return pltpu.make_async_remote_copy(
            src_ref=src,
            dst_ref=dst,
            send_sem=send,
            recv_sem=recv,
            device_id={axis: target},
            device_id_type=pl.DeviceIdType.MESH,
        )

    def weight_copies(target, source):
        return [
            across("section", target, ref.at[source], ref.at[source], wsend.at[target, i], wrecv.at[source, i])
            for i, ref in enumerate((taps_raw, w1_ref, w2_ref))
        ]

    def z_copy(target, source):
        return across("section", target, zst.at[target], zrec.at[source], zsend.at[target], zrecv.at[source])

    def g_copy(target, source):
        return across("section", target, gst.at[target], grec.at[source], gsend.at[target], grecv.at[source])

    def part_copy(l, target, source):
        i = lax.rem(l, blocks)
        return across("section", target, part.at[l], arec.at[source, i], asend.at[l], arecv.at[source, i])

    def restored(v16):
        out_field[...] = packed(mm(perm_ref[...], unpacked(v16), ((0,), (0,))))
        columns = [out_field[pl.ds(k, 16, stride=8), :] for k in range(8)]
        return jnp.concatenate(columns, axis=1).astype(bf16)

    def taken(v):
        v = v.astype(f32)
        for k in range(8):
            out_field[pl.ds(k, 16, stride=8), :] = v[:, 128 * k : 128 * k + 128]
        rows16 = unpacked(out_field[...].astype(bf16))
        return packed(mm(perm_ref[...], rows16, ((1,), (0,))))

    offsets = grid_offsets(tile_count)
    north, east, south, west, ne, se, sw, nw = [
        lax.rem(me + (off % tile_count), tile_count) for off in offsets
    ]

    def copies(plan, recv):
        return [
            pltpu.make_async_remote_copy(
                src_ref=src,
                dst_ref=dst,
                send_sem=send_sem.at[i],
                recv_sem=recv.at[i],
                device_id={"tile": target},
                device_id_type=pl.DeviceIdType.MESH,
            )
            for i, (target, src, dst) in enumerate(plan)
        ]

    def forward_copies(l):
        return copies(
            [
                (north, pad.at[l, 3:6, 8:16], pad.at[l, 19:22, 8:16]),
                (south, pad.at[l, 16:19, 8:16], pad.at[l, 0:3, 8:16]),
                (nw, es.at[WEST, :, 0:8], fr.at[l, EAST, :, 24:32]),
                (ne, es.at[EAST, :, 0:8], fr.at[l, WEST, :, 24:32]),
                (se, es.at[EAST, :, 8:16], fr.at[l, WEST, :, 0:8]),
                (sw, es.at[WEST, :, 8:16], fr.at[l, EAST, :, 0:8]),
                (east, es.at[EAST], fr.at[l, WEST, :, 8:24]),
                (west, es.at[WEST], fr.at[l, EAST, :, 8:24]),
            ],
            frecv.at[l],
        )

    def backward_copies(l):
        return copies(
            [
                (north, dp.at[0:3, 8:16], bn.at[l, 1]),
                (south, dp.at[19:22, 8:16], bn.at[l, 0]),
                (nw, eb.at[WEST, :, 0:8], br.at[l, EAST, :, 24:32]),
                (ne, eb.at[EAST, :, 0:8], br.at[l, WEST, :, 24:32]),
                (se, eb.at[EAST, :, 24:32], br.at[l, WEST, :, 16:24]),
                (sw, eb.at[WEST, :, 24:32], br.at[l, EAST, :, 16:24]),
                (east, eb.at[EAST, :, 8:24], br.at[l, WEST, :, 0:16]),
                (west, eb.at[WEST, :, 8:24], br.at[l, EAST, :, 0:16]),
            ],
            brecv.at[l],
        )

    def offer(l, z):
        pad[l, 3:19, 8:16, :] = z.reshape(16, 8, 128)
        field[...] = z
        for pair in range(2):
            es[WEST, pair] = field[pl.ds(pair, 16, stride=8), :]
            es[EAST, pair] = field[pl.ds(6 + pair, 16, stride=8), :]

    barrier = pltpu.get_barrier_semaphore()

    def greet(j, carry):
        pl.semaphore_signal(
            barrier,
            inc=1,
            device_id={"tile": lax.rem(me + j, tile_count)},
            device_id_type=pl.DeviceIdType.MESH,
        )
        return carry

    lax.fori_loop(1, tile_count, greet, 0)
    for other in others:
        pl.semaphore_signal(
            barrier,
            inc=1,
            device_id={"section": other},
            device_id_type=pl.DeviceIdType.MESH,
        )
    code = orientation_ref[me]
    back_code = lax.rem(4 - code, 4)
    missing_ne = jnp.where(neighbour_ref[0, 4 + back_code] < 0, 1, 0)
    missing_sw = jnp.where(neighbour_ref[0, 4 + lax.rem(6 - code, 4)] < 0, 1, 0)
    row = lax.broadcasted_iota(jnp.int32, (22, 128), 0)
    mask_ref[WEST] = jnp.where((row >= 19) & (missing_sw > 0), 0.0, 1.0)
    mask_ref[EAST] = jnp.where((row < 3) & (missing_ne > 0), 0.0, 1.0)

    def natural(count, axis):
        i = lax.broadcasted_iota(jnp.int32, (count, count), axis)
        return (i & 127) * 2 + (i >> 7)

    perm_ref[...] = turned(16, back_code, natural(256, 0), natural(256, 1))
    first = lax.broadcasted_iota(jnp.int32, (64, 64), 0)
    second = lax.broadcasted_iota(jnp.int32, (64, 64), 1)
    tap_turn = turned(side, back_code, first, second)
    tap_perm_ref[...] = jnp.where((first < 49) & (second < 49), tap_turn, jnp.zeros_like(tap_turn))
    dk_ref[...] = jnp.zeros_like(dk_ref)
    for i in range(blocks):
        own = taps_own[i].astype(f32)
        dk_ref[0:49, :] = jnp.concatenate([own, own], axis=1)
        taps_raw[mine, i] = dk_ref[...].astype(bf16)
    w1_ref[mine] = w1_own[...]
    w2_ref[mine] = w2_own[...]
    offer(0, taken(x_ref[mine, 0]))
    rims[...] = jnp.zeros_like(rims)
    rows = lax.broadcasted_iota(jnp.int32, (256, 128), 0)
    lanes = lax.broadcasted_iota(jnp.int32, (256, 128), 1)
    same = ((rows % 128) < 64) == (lanes < 64)
    averaging[...] = jnp.where(same, 1.0 / 64.0, 0.0).astype(bf16)
    dz[...] = jnp.zeros_like(dz)
    dodd[...] = jnp.zeros_like(dodd)
    eb[...] = jnp.zeros_like(eb)
    pl.semaphore_wait(barrier, tile_count - 1 + sections - 1)
    for copy in forward_copies(0):
        copy.start()
    for other in others:
        for copy in weight_copies(other, mine):
            copy.start()
    grad[...] = taken(ct_ref[mine, 0])
    total_ref[...] = jnp.zeros_like(total_ref)

    def low_lanes(shape):
        return lax.broadcasted_iota(jnp.int32, shape, len(shape) - 1) < 64

    def forward_step(l, carry):
        sec, block = l // blocks, lax.rem(l, blocks)

        @pl.when((block == 0) & (sec != mine))
        def _():
            for copy in weight_copies(mine, sec):
                copy.wait_recv()

        taps_ref[l] = mm(tap_perm_ref[...], taps_raw[sec, block], ((1,), (0,)))
        sent = forward_copies(l)
        for copy in sent:
            copy.wait_recv()
        for edge in range(2):
            for pair in range(2):
                column = fr[l, edge, pair, 5:27, :] * mask_ref[edge]
                place = (6 if edge == WEST else 16) + pair
                pad[l, :, place : place + 1, :] = column.reshape(22, 1, 128)
        keep = low_lanes((22, 16, 128))
        merged = jnp.where(keep, pad[l, :, 7:23, :], pad[l, :, 6:22, :])
        odd[l] = pltpu.roll(merged.reshape(22 * 16, 128), 64, 1).reshape(22, 16, 128)
        total = jnp.zeros((16, 8, 128), f32)
        for a in range(side):
            for b in range(side):
                if b % 2:
                    start = 6 + (b + 1) // 2
                    window = pad[l, a : a + 16, start : start + 8, :]
                else:
                    window = odd[l, a : a + 16, b // 2 : b // 2 + 8, :]
                total = total + window * taps_ref[l, side * a + b]
        h = total.reshape(128, 128)
        avg = averaging[...]
        centred = h - half_mean(h, avg)
        scale = lax.rsqrt(half_mean(centred * centred, avg) + norm_eps)
        normed = centred * scale
        xhat[l] = normed
        inv[l] = scale
        u = unpacked(normed.astype(bf16))
        us[l] = u
        before = mm(u, w1_ref[sec, block], ((1,), (0,)))
        t = jnp.tanh(gelu_k * (before + gelu_c * before * before * before))
        g = (0.5 * before * (1.0 + t)).astype(bf16)
        gs[l] = g
        branch = packed(mm(g, w2_ref[sec, block], ((1,), (0,))))
        z = pad[l, 3:19, 8:16, :].reshape(128, 128) + branch
        z16 = z.astype(bf16)
        for copy in sent:
            copy.wait_send()

        @pl.when(l < layers - 1)
        def _():
            offer(l + 1, z16.astype(f32))
            for copy in forward_copies(l + 1):
                copy.start()

        square = before * before
        @pl.when(block == blocks - 1)
        def _():
            zst[sec] = restored(z16)

        @pl.when((block == blocks - 1) & (sec != mine))
        def _():
            z_copy(sec, mine).start()

        slope[l] = 0.5 * (1.0 + t) + 0.5 * before * (1.0 - t * t) * gelu_k * (
            1.0 + 3.0 * gelu_c * square
        )
        return carry

    lax.fori_loop(0, layers, forward_step, 0)

    def backward_step(count, carry):
        l = layers - 1 - count
        sec, block = l // blocks, lax.rem(l, blocks)
        d = grad[...]
        d_rows = unpacked(d.astype(bf16))
        dg = mm(d_rows, w2_ref[sec, block], ((1,), (1,)))
        da = (dg * slope[l]).astype(bf16)
        du = packed(mm(da, w1_ref[sec, block], ((1,), (1,))))
        avg = averaging[...]
        normed = xhat[l]
        dh = inv[l] * (du - half_mean(du, avg) - normed * half_mean(du * normed, avg))
        dh3 = dh.reshape(16, 8, 128)
        dz[6:22, 8:16, :] = dh3
        keep = low_lanes((16, 8, 128))
        for start in (0, 8):
            merged = jnp.where(
                keep, dz[6:22, start + 1 : start + 9, :], dz[6:22, start : start + 8, :]
            )
            rolled = pltpu.roll(merged.reshape(128, 128), 64, 1).reshape(16, 8, 128)
            dodd[6:22, start : start + 8, :] = rolled
        for top in (0, 19):
            total = [jnp.zeros((16, 128), f32) for _ in range(3)]
            for b in range(side):
                shift = 3 - b
                ref = dodd if shift % 2 else dz
                start = 6 + shift // 2
                for q in range(3):
                    for a in range(side):
                        if not 0 <= top + q - a <= 15:
                            continue
                        window = ref[top + q + 6 - a, start : start + 16, :]
                        total[q] = total[q] + window * taps_ref[l, side * a + b]
            for q in range(3):
                dp[top + q, 6:22, :] = total[q]
        sources = (((dz, 8), (dodd, 7), (dodd, 8)), ((dz, 15), (dodd, 15), (dodd, 14)))
        for edge in range(2):
            for k, (ref, pair) in enumerate(sources[edge]):
                rims[edge, k, 6:22, :] = ref[6:22, pair : pair + 1, :].reshape(16, 128)
        uses = (
            ((0, 0, 1), (1, 0, 2), (1, 1, 0), (1, 2, 1)),
            ((0, 4, 1), (0, 5, 0), (0, 6, 2), (1, 6, 1)),
        )
        for edge in range(2):
            total = [jnp.zeros((22, 128), f32) for _ in range(2)]
            for pair, b, k in uses[edge]:
                for a in range(side):
                    window = rims[edge, k, 6 - a : 28 - a, :]
                    total[pair] = total[pair] + window * taps_ref[l, side * a + b]
            for pair in range(2):
                eb[edge, pair, 5:27, :] = total[pair] * mask_ref[edge]
        sent = backward_copies(l)
        for copy in sent:
            copy.start()

        centre = jnp.zeros((16, 8, 128), f32)
        for a in range(side):
            for b in range(side):
                shift = 3 - b
                ref = dodd if shift % 2 else dz
                start = 8 + shift // 2
                window = ref[9 - a : 25 - a, start : start + 8, :]
                centre = centre + window * taps_ref[l, side * a + b]
        grad[...] = d + centre.reshape(128, 128)

        for a in range(side):
            for b in range(side):
                if b % 2:
                    start = 6 + (b + 1) // 2
                    window = pad[l, a : a + 16, start : start + 8, :]
                else:
                    window = odd[l, a : a + 16, b // 2 : b // 2 + 8, :]
                tap_rows = jnp.sum(window * dh3, axis=0)
                dk_ref[side * a + b : side * a + b + 1, :] = jnp.sum(
                    tap_rows, axis=0, keepdims=True
                )
        grad_in = mm(us[l], da, ((0,), (0,)))
        grad_out = mm(gs[l], d_rows, ((0,), (0,)))

        part[l, 0:128] = jnp.concatenate([grad_in[:, :128], grad_in[:, 128:]], axis=0).astype(bf16)
        part[l, 128:256] = packed(grad_out).astype(bf16)
        tap_sums = dk_ref[...]
        high = tap_sums.astype(bf16)
        low = (tap_sums - high.astype(f32)).astype(bf16)
        turn = tap_perm_ref[...]
        part[l, 256:320] = (mm(turn, high, ((0,), (0,))) + mm(turn, low, ((0,), (0,)))).astype(bf16)

        @pl.when(sec != mine)
        def _():
            part_copy(l, sec, mine).start()

        for copy in sent:
            copy.wait_recv()
        base = grad[...].reshape(16, 8, 128)
        top_part = base[0:3] + bn[l, 0]
        bottom_part = base[13:16] + bn[l, 1]
        field[...] = jnp.concatenate([top_part, base[3:13], bottom_part], axis=0).reshape(128, 128)
        for edge in range(2):
            for pair in range(2):
                place = (0 if edge == WEST else 6) + pair
                extra = br[l, edge, pair, 0:16, :] + br[l, edge, pair, 16:32, :]
                field[pl.ds(place, 16, stride=8), :] = (
                    field[pl.ds(place, 16, stride=8), :] + extra
                )
        result = field[...].astype(bf16)
        grad[...] = result.astype(f32)

        @pl.when(block == 0)
        def _():
            gst[sec] = restored(result)

        @pl.when((block == 0) & (sec != mine))
        def _():
            g_copy(sec, mine).start()

        for copy in sent:
            copy.wait_send()
        return carry

    lax.fori_loop(0, layers, backward_step, 0)

    for i in range(blocks):
        total = part[mine * blocks + i].astype(f32)
        for other in others:
            part_copy(mine * blocks + i, mine, other).wait_recv()
            total = total + arec[other, i].astype(f32)
        total_ref[320 * i : 320 * i + 320] = total.astype(bf16)

    def place(tile):
        return pl.ds(pl.multiple_of(tile * piece, 16), piece)

    def ahead(j):
        return lax.rem(me + j, tile_count)

    def behind(j):
        return lax.rem(me + tile_count - j, tile_count)

    def scatter(j, tile):
        return across("tile", tile, total_ref.at[place(tile)], rs.at[j], rsend.at[j], rrecv.at[j])

    def spread(j, tile, source):
        spot = place(source)
        return across("tile", tile, fin.at[spot], fin.at[spot], csend.at[j], crecv.at[j])

    def each(body):
        def step(j, carry):
            body(j)
            return carry

        lax.fori_loop(1, tile_count, step, 0)

    each(lambda j: scatter(j, ahead(j)).start())

    def gathered(j, total):
        scatter(j, ahead(j)).wait_recv()
        return total + rs[j].astype(f32)

    total = lax.fori_loop(1, tile_count, gathered, total_ref[place(me)].astype(f32))
    fin[place(me)] = (total * grad_scale).astype(bf16)
    each(lambda j: spread(j, ahead(j), me).start())

    zo_ref[0, mine, 0] = zst[mine]
    go_ref[0, mine, 0] = gst[mine]
    for other in others:
        z_copy(mine, other).wait_recv()
        zo_ref[0, other, 0] = zrec[other]
        g_copy(mine, other).wait_recv()
        go_ref[0, other, 0] = grec[other]
    for other in others:
        for copy in weight_copies(other, mine):
            copy.wait_send()
        z_copy(other, mine).wait_send()
        g_copy(other, mine).wait_send()
        for i in range(blocks):
            part_copy(other * blocks + i, other, mine).wait_send()
    each(lambda j: scatter(j, ahead(j)).wait_send())
    each(lambda j: spread(j, me, behind(j)).wait_recv())
    each(lambda j: spread(j, ahead(j), me).wait_send())
    for i in range(blocks):
        whole = fin[320 * i : 320 * i + 320].astype(f32)
        dw1_out[i] = jnp.concatenate([whole[0:64], whole[64:128]], axis=1)
        dw2_out[i] = unpacked(whole[128:256])
        dk_out[i] = whole[256:305, :64] + whole[256:305, 64:]


def on_device(inputs, cotangent, depth_weight, in_weight, out_weight, neighbours, orientation):
    micro_count, _, extent, merged = inputs.shape
    blocks, taps, channels = depth_weight.shape
    hidden = in_weight.shape[2]
    tile_count = lax.axis_size("tile")
    sections = lax.axis_size("section")
    layers = blocks * sections
    grad_scale = 1.0 / math.sqrt(micro_count * tile_count * extent * extent)
    piece = -(-320 * blocks // (16 * tile_count)) * 16

    vmem = pl.BlockSpec(memory_space=pltpu.VMEM)
    smem = pl.BlockSpec(memory_space=pltpu.SMEM)
    zo, go, dk, dw1, dw2 = pl.pallas_call(
        functools.partial(kernel, tile_count, sections, blocks, piece, grad_scale),
        out_shape=(
            jax.ShapeDtypeStruct((1, micro_count, 1, extent, merged), bf16),
            jax.ShapeDtypeStruct((1, micro_count, 1, extent, merged), bf16),
            jax.ShapeDtypeStruct((blocks, taps, channels), f32),
            jax.ShapeDtypeStruct((blocks, channels, hidden), f32),
            jax.ShapeDtypeStruct((blocks, hidden, channels), f32),
        ),
        in_specs=[vmem] * 5 + [smem] * 2,
        out_specs=(vmem,) * 5,
        scratch_shapes=[
            pltpu.VMEM((2, 22, 128), f32),
            pltpu.VMEM((256, 256), bf16),
            pltpu.VMEM((64, 64), bf16),
            pltpu.VMEM((2, 3, 32, 128), f32),
            pltpu.VMEM((sections, blocks, 64, 128), bf16),
            pltpu.VMEM((layers, 64, 128), f32),
            pltpu.VMEM((sections, blocks, channels, hidden), bf16),
            pltpu.VMEM((sections, blocks, hidden, channels), bf16),
            pltpu.VMEM((sections, 16, 1024), bf16),
            pltpu.VMEM((sections, 16, 1024), bf16),
            pltpu.VMEM((sections, 16, 1024), bf16),
            pltpu.VMEM((sections, 16, 1024), bf16),
            pltpu.VMEM((128, 128), f32),
            pltpu.VMEM((64, 128), f32),
            pltpu.VMEM((layers, 320, 128), bf16),
            pltpu.VMEM((sections, blocks, 320, 128), bf16),
            pltpu.VMEM((piece * tile_count, 128), bf16),
            pltpu.VMEM((tile_count, piece, 128), bf16),
            pltpu.VMEM((piece * tile_count, 128), bf16),
            pltpu.VMEM((layers, 22, 24, 128), f32),
            pltpu.VMEM((layers, 22, 16, 128), f32),
            pltpu.VMEM((2, 2, 16, 128), f32),
            pltpu.VMEM((layers, 2, 2, 32, 128), f32),
            pltpu.VMEM((layers, 128, 128), f32),
            pltpu.VMEM((layers, 128, 128), f32),
            pltpu.VMEM((layers, 256, 64), bf16),
            pltpu.VMEM((layers, 256, 256), bf16),
            pltpu.VMEM((layers, 256, 256), f32),
            pltpu.VMEM((28, 24, 128), f32),
            pltpu.VMEM((28, 24, 128), f32),
            pltpu.VMEM((22, 24, 128), f32),
            pltpu.VMEM((2, 2, 32, 128), f32),
            pltpu.VMEM((layers, 2, 2, 32, 128), f32),
            pltpu.VMEM((layers, 2, 3, 8, 128), f32),
            pltpu.VMEM((128, 128), f32),
            pltpu.VMEM((128, 128), f32),
            pltpu.VMEM((256, 128), bf16),
            pltpu.SemaphoreType.DMA((8,)),
            pltpu.SemaphoreType.DMA((layers, 8)),
            pltpu.SemaphoreType.DMA((layers, 8)),
            pltpu.SemaphoreType.DMA((sections, 3)),
            pltpu.SemaphoreType.DMA((sections, 3)),
            pltpu.SemaphoreType.DMA((sections,)),
            pltpu.SemaphoreType.DMA((sections,)),
            pltpu.SemaphoreType.DMA((sections,)),
            pltpu.SemaphoreType.DMA((sections,)),
            pltpu.SemaphoreType.DMA((layers,)),
            pltpu.SemaphoreType.DMA((sections, blocks)),
            pltpu.SemaphoreType.DMA((tile_count,)),
            pltpu.SemaphoreType.DMA((tile_count,)),
            pltpu.SemaphoreType.DMA((tile_count,)),
            pltpu.SemaphoreType.DMA((tile_count,)),
        ],
        compiler_params=pltpu.CompilerParams(
            collective_id=0, has_side_effects=True, vmem_limit_bytes=40 * 1024 * 1024
        ),
    )(inputs, cotangent, depth_weight, in_weight, out_weight, neighbours, orientation)
    return (zo, go, dk, dw1, dw2)


def solution(mesh):
    in_specs = (
        P(None, "tile", None, None),
        P(None, "tile", None, None),
        P("section", None, None),
        P("section", None, None),
        P("section", None, None),
        P("tile", None),
        P(),
    )
    out_specs = (
        P("section", None, "tile", None, None),
        P("section", None, "tile", None, None),
        P("section", None, None),
        P("section", None, None),
        P("section", None, None),
    )
    return jax.shard_map(
        on_device, mesh=mesh, in_specs=in_specs, out_specs=out_specs, check_vma=False
    )
```

```python
import functools
import math

import jax
import jax.numpy as jnp
from jax import lax
from jax.experimental import pallas as pl
from jax.experimental.pallas import tpu as pltpu
from jax.sharding import PartitionSpec as P

norm_eps = 1e-06
rim = 3
side = 7
gelu_k = math.sqrt(2.0 / math.pi)
gelu_c = 0.044715
f32, bf16 = jnp.float32, jnp.bfloat16
WEST, EAST = 0, 1


def grid_offsets(tile_count):
    columns = max(tile_count // 8, 4)
    return [-columns, 1, columns, -1, 1 - columns, columns + 1, columns - 1, -columns - 1]


def unpacked(v):
    half = v.shape[1] // 2
    return jnp.concatenate([v[:, :half], v[:, half:]], axis=0)


def packed(v):
    half = v.shape[0] // 2
    return jnp.concatenate([v[:half], v[half:]], axis=1)


def mm(a, b, dims):
    return lax.dot_general(a, b, ((dims[0], dims[1]), ((), ())), preferred_element_type=f32)


def half_mean(v, averaging):
    high = v.astype(bf16)
    low = (v - high.astype(f32)).astype(bf16)
    return mm(jnp.concatenate([high, low], axis=1), averaging, ((1,), (0,)))


def turned(n, code, place, cell):
    r, c = place // n, place % n
    source = place
    for k, choice in ((1, c * n + n - 1 - r), (2, n * n - 1 - place), (3, (n - 1 - c) * n + r)):
        source = jnp.where(code == k, choice, source)
    return jnp.where(source == cell, 1.0, 0.0).astype(bf16)


def kernel(
    tile_count,
    sections,
    blocks,
    piece,
    grad_scale,
    x_ref,
    ct_ref,
    taps_own,
    w1_own,
    w2_own,
    neighbour_ref,
    orientation_ref,
    zo_ref,
    go_ref,
    dk_out,
    dw1_out,
    dw2_out,
    mask_ref,
    perm_ref,
    tap_perm_ref,
    rims,
    taps_raw,
    taps_ref,
    w1_ref,
    w2_ref,
    zst,
    gst,
    zrec,
    grec,
    out_field,
    dk_ref,
    part,
    arec,
    total_ref,
    rs,
    fin,
    pad,
    odd,
    rows_out,
    edge_out,
    corner_out,
    rows_in,
    edge_in,
    corner_in,
    fr,
    xhat,
    inv,
    us,
    gs,
    slope,
    dz,
    dodd,
    dp,
    eb,
    field,
    grad,
    averaging,
    send_sem,
    frecv,
    brecv,
    wsend,
    wrecv,
    zsend,
    zrecv,
    gsend,
    grecv,
    asend,
    arecv,
    rsend,
    rrecv,
    csend,
    crecv,
):
    layers = sections * blocks
    me = lax.axis_index("tile")
    mine = lax.axis_index("section")
    others = [lax.rem(mine + k, sections) for k in range(1, sections)]

    def across(axis, target, src, dst, send, recv):
        return pltpu.make_async_remote_copy(
            src_ref=src,
            dst_ref=dst,
            send_sem=send,
            recv_sem=recv,
            device_id={axis: target},
            device_id_type=pl.DeviceIdType.MESH,
        )

    def weight_copies(target, source):
        return [
            across("section", target, ref.at[source], ref.at[source], wsend.at[target, i], wrecv.at[source, i])
            for i, ref in enumerate((taps_raw, w1_ref, w2_ref))
        ]

    def z_copy(target, source):
        return across("section", target, zst.at[target], zrec.at[source], zsend.at[target], zrecv.at[source])

    def g_copy(target, source):
        return across("section", target, gst.at[target], grec.at[source], gsend.at[target], grecv.at[source])

    def part_copy(l, target, source):
        i = lax.rem(l, blocks)
        return across("section", target, part.at[l], arec.at[source, i], asend.at[l], arecv.at[source, i])

    def restored(v16):
        out_field[...] = packed(mm(perm_ref[...], unpacked(v16), ((0,), (0,))))
        columns = [out_field[pl.ds(k, 16, stride=8), :] for k in range(8)]
        return jnp.concatenate(columns, axis=1).astype(bf16)

    def taken(v):
        v = v.astype(f32)
        for k in range(8):
            out_field[pl.ds(k, 16, stride=8), :] = v[:, 128 * k : 128 * k + 128]
        rows16 = unpacked(out_field[...].astype(bf16))
        return packed(mm(perm_ref[...], rows16, ((1,), (0,))))

    offsets = grid_offsets(tile_count)
    north, east, south, west, ne, se, sw, nw = [
        lax.rem(me + (off % tile_count), tile_count) for off in offsets
    ]

    def copies(plan, recv):
        return [
            pltpu.make_async_remote_copy(
                src_ref=src,
                dst_ref=dst,
                send_sem=send_sem.at[i],
                recv_sem=recv.at[i],
                device_id={"tile": target},
                device_id_type=pl.DeviceIdType.MESH,
            )
            for i, (target, src, dst) in enumerate(plan)
        ]

    def halo_copies(slot, recv):
        return copies(
            [
                (north, rows_out.at[0], rows_in.at[slot, 1]),
                (south, rows_out.at[1], rows_in.at[slot, 0]),
                (nw, corner_out.at[WEST, 0], corner_in.at[slot, EAST, 1]),
                (ne, corner_out.at[EAST, 0], corner_in.at[slot, WEST, 1]),
                (se, corner_out.at[EAST, 1], corner_in.at[slot, WEST, 0]),
                (sw, corner_out.at[WEST, 1], corner_in.at[slot, EAST, 0]),
                (east, edge_out.at[EAST], edge_in.at[slot, WEST]),
                (west, edge_out.at[WEST], edge_in.at[slot, EAST]),
            ],
            recv,
        )

    def forward_copies(l):
        return halo_copies(l, frecv.at[l])

    def backward_copies(l):
        return halo_copies(layers + l, brecv.at[l])

    def joined(*parts):
        return jnp.concatenate(parts, axis=0).astype(bf16)

    def offer(l, z):
        z3 = z.reshape(16, 8, 128)
        pad[l, 3:19, 8:16, :] = z3
        field[...] = z
        rows_out[0] = z[0:32].astype(bf16)
        rows_out[1] = z[96:128].astype(bf16)
        for edge, base in ((WEST, 0), (EAST, 6)):
            one = field[pl.ds(base, 16, stride=8), :]
            two = field[pl.ds(base + 1, 16, stride=8), :]
            edge_out[edge] = joined(one, two)
            corner_out[edge, 0] = joined(one[0:8], two[0:8])
            corner_out[edge, 1] = joined(one[8:16], two[8:16])

    barrier = pltpu.get_barrier_semaphore()

    def greet(j, carry):
        pl.semaphore_signal(
            barrier,
            inc=1,
            device_id={"tile": lax.rem(me + j, tile_count)},
            device_id_type=pl.DeviceIdType.MESH,
        )
        return carry

    lax.fori_loop(1, tile_count, greet, 0)
    for other in others:
        pl.semaphore_signal(
            barrier,
            inc=1,
            device_id={"section": other},
            device_id_type=pl.DeviceIdType.MESH,
        )
    code = orientation_ref[me]
    back_code = lax.rem(4 - code, 4)
    missing_ne = jnp.where(neighbour_ref[0, 4 + back_code] < 0, 1, 0)
    missing_sw = jnp.where(neighbour_ref[0, 4 + lax.rem(6 - code, 4)] < 0, 1, 0)
    row = lax.broadcasted_iota(jnp.int32, (22, 128), 0)
    mask_ref[WEST] = jnp.where((row >= 19) & (missing_sw > 0), 0.0, 1.0)
    mask_ref[EAST] = jnp.where((row < 3) & (missing_ne > 0), 0.0, 1.0)

    def natural(count, axis):
        i = lax.broadcasted_iota(jnp.int32, (count, count), axis)
        return (i & 127) * 2 + (i >> 7)

    perm_ref[...] = turned(16, back_code, natural(256, 0), natural(256, 1))
    first = lax.broadcasted_iota(jnp.int32, (64, 64), 0)
    second = lax.broadcasted_iota(jnp.int32, (64, 64), 1)
    tap_turn = turned(side, back_code, first, second)
    tap_perm_ref[...] = jnp.where((first < 49) & (second < 49), tap_turn, jnp.zeros_like(tap_turn))
    dk_ref[...] = jnp.zeros_like(dk_ref)
    for i in range(blocks):
        own = taps_own[i].astype(f32)
        dk_ref[0:49, :] = jnp.concatenate([own, own], axis=1)
        taps_raw[mine, i] = dk_ref[...].astype(bf16)
    w1_ref[mine] = w1_own[...]
    w2_ref[mine] = w2_own[...]
    offer(0, taken(x_ref[mine, 0]))
    rims[...] = jnp.zeros_like(rims)
    rows = lax.broadcasted_iota(jnp.int32, (256, 128), 0)
    lanes = lax.broadcasted_iota(jnp.int32, (256, 128), 1)
    same = ((rows % 128) < 64) == (lanes < 64)
    averaging[...] = jnp.where(same, 1.0 / 64.0, 0.0).astype(bf16)
    dz[...] = jnp.zeros_like(dz)
    dodd[...] = jnp.zeros_like(dodd)
    eb[...] = jnp.zeros_like(eb)
    dp[...] = jnp.zeros_like(dp)
    pl.semaphore_wait(barrier, tile_count - 1 + sections - 1)
    for copy in forward_copies(0):
        copy.start()
    for other in others:
        for copy in weight_copies(other, mine):
            copy.start()
    grad[...] = taken(ct_ref[mine, 0])
    total_ref[...] = jnp.zeros_like(total_ref)

    def low_lanes(shape):
        return lax.broadcasted_iota(jnp.int32, shape, len(shape) - 1) < 64

    def forward_step(l, carry):
        sec, block = l // blocks, lax.rem(l, blocks)

        @pl.when((block == 0) & (sec != mine))
        def _():
            for copy in weight_copies(mine, sec):
                copy.wait_recv()

        taps_ref[l] = mm(tap_perm_ref[...], taps_raw[sec, block], ((1,), (0,)))
        sent = forward_copies(l)
        for copy in sent:
            copy.wait_recv()
        pad[l, 0:3, 8:16, :] = rows_in[l, 0].astype(f32).reshape(4, 8, 128)[1:4]
        pad[l, 19:22, 8:16, :] = rows_in[l, 1].astype(f32).reshape(4, 8, 128)[0:3]
        for edge in range(2):
            sides = edge_in[l, edge].astype(f32)
            upper = corner_in[l, edge, 0].astype(f32)
            lower = corner_in[l, edge, 1].astype(f32)
            for pair in range(2):
                fr[edge, pair, 0:8] = upper[8 * pair : 8 * pair + 8]
                fr[edge, pair, 8:24] = sides[16 * pair : 16 * pair + 16]
                fr[edge, pair, 24:32] = lower[8 * pair : 8 * pair + 8]
                column = fr[edge, pair, 5:27, :] * mask_ref[edge]
                place = (6 if edge == WEST else 16) + pair
                pad[l, :, place : place + 1, :] = column.reshape(22, 1, 128)
        keep = low_lanes((22, 16, 128))
        merged = jnp.where(keep, pad[l, :, 7:23, :], pad[l, :, 6:22, :])
        odd[l] = pltpu.roll(merged.reshape(22 * 16, 128), 64, 1).reshape(22, 16, 128)
        total = jnp.zeros((16, 8, 128), f32)
        for a in range(side):
            for b in range(side):
                if b % 2:
                    start = 6 + (b + 1) // 2
                    window = pad[l, a : a + 16, start : start + 8, :]
                else:
                    window = odd[l, a : a + 16, b // 2 : b // 2 + 8, :]
                total = total + window * taps_ref[l, side * a + b]
        h = total.reshape(128, 128)
        avg = averaging[...]
        centred = h - half_mean(h, avg)
        scale = lax.rsqrt(half_mean(centred * centred, avg) + norm_eps)
        normed = centred * scale
        xhat[l] = normed
        inv[l] = scale
        u = unpacked(normed.astype(bf16))
        us[l] = u
        before = mm(u, w1_ref[sec, block], ((1,), (0,)))
        t = jnp.tanh(gelu_k * (before + gelu_c * before * before * before))
        g = (0.5 * before * (1.0 + t)).astype(bf16)
        gs[l] = g
        branch = packed(mm(g, w2_ref[sec, block], ((1,), (0,))))
        z = pad[l, 3:19, 8:16, :].reshape(128, 128) + branch
        z16 = z.astype(bf16)
        for copy in sent:
            copy.wait_send()

        @pl.when(l < layers - 1)
        def _():
            offer(l + 1, z16.astype(f32))
            for copy in forward_copies(l + 1):
                copy.start()

        square = before * before
        @pl.when(block == blocks - 1)
        def _():
            zst[sec] = restored(z16)

        @pl.when((block == blocks - 1) & (sec != mine))
        def _():
            z_copy(sec, mine).start()

        slope[l] = 0.5 * (1.0 + t) + 0.5 * before * (1.0 - t * t) * gelu_k * (
            1.0 + 3.0 * gelu_c * square
        )
        return carry

    lax.fori_loop(0, layers, forward_step, 0)

    def backward_step(count, carry):
        l = layers - 1 - count
        sec, block = l // blocks, lax.rem(l, blocks)
        d = grad[...]
        d_rows = unpacked(d.astype(bf16))
        dg = mm(d_rows, w2_ref[sec, block], ((1,), (1,)))
        da = (dg * slope[l]).astype(bf16)
        du = packed(mm(da, w1_ref[sec, block], ((1,), (1,))))
        avg = averaging[...]
        normed = xhat[l]
        dh = inv[l] * (du - half_mean(du, avg) - normed * half_mean(du * normed, avg))
        dh3 = dh.reshape(16, 8, 128)
        dz[6:22, 8:16, :] = dh3
        keep = low_lanes((16, 8, 128))
        for start in (0, 8):
            merged = jnp.where(
                keep, dz[6:22, start + 1 : start + 9, :], dz[6:22, start : start + 8, :]
            )
            rolled = pltpu.roll(merged.reshape(128, 128), 64, 1).reshape(16, 8, 128)
            dodd[6:22, start : start + 8, :] = rolled
        for top in (0, 19):
            total = [jnp.zeros((16, 128), f32) for _ in range(3)]
            for b in range(side):
                shift = 3 - b
                ref = dodd if shift % 2 else dz
                start = 6 + shift // 2
                for q in range(3):
                    for a in range(side):
                        if not 0 <= top + q - a <= 15:
                            continue
                        window = ref[top + q + 6 - a, start : start + 16, :]
                        total[q] = total[q] + window * taps_ref[l, side * a + b]
            for q in range(3):
                dp[top + q, 6:22, :] = total[q]
        sources = (((dz, 8), (dodd, 7), (dodd, 8)), ((dz, 15), (dodd, 15), (dodd, 14)))
        for edge in range(2):
            for k, (ref, pair) in enumerate(sources[edge]):
                rims[edge, k, 6:22, :] = ref[6:22, pair : pair + 1, :].reshape(16, 128)
        uses = (
            ((0, 0, 1), (1, 0, 2), (1, 1, 0), (1, 2, 1)),
            ((0, 4, 1), (0, 5, 0), (0, 6, 2), (1, 6, 1)),
        )
        for edge in range(2):
            total = [jnp.zeros((22, 128), f32) for _ in range(2)]
            for pair, b, k in uses[edge]:
                for a in range(side):
                    window = rims[edge, k, 6 - a : 28 - a, :]
                    total[pair] = total[pair] + window * taps_ref[l, side * a + b]
            for pair in range(2):
                eb[edge, pair, 5:27, :] = total[pair] * mask_ref[edge]
        rows_out[0] = dp[0:4, 8:16, :].reshape(32, 128).astype(bf16)
        rows_out[1] = dp[18:22, 8:16, :].reshape(32, 128).astype(bf16)
        for edge in range(2):
            edge_out[edge] = joined(eb[edge, 0, 8:24], eb[edge, 1, 8:24])
            corner_out[edge, 0] = joined(eb[edge, 0, 0:8], eb[edge, 1, 0:8])
            corner_out[edge, 1] = joined(eb[edge, 0, 24:32], eb[edge, 1, 24:32])
        sent = backward_copies(l)
        for copy in sent:
            copy.start()

        centre = jnp.zeros((16, 8, 128), f32)
        for a in range(side):
            for b in range(side):
                shift = 3 - b
                ref = dodd if shift % 2 else dz
                start = 8 + shift // 2
                window = ref[9 - a : 25 - a, start : start + 8, :]
                centre = centre + window * taps_ref[l, side * a + b]
        grad[...] = d + centre.reshape(128, 128)

        for a in range(side):
            for b in range(side):
                if b % 2:
                    start = 6 + (b + 1) // 2
                    window = pad[l, a : a + 16, start : start + 8, :]
                else:
                    window = odd[l, a : a + 16, b // 2 : b // 2 + 8, :]
                tap_rows = jnp.sum(window * dh3, axis=0)
                dk_ref[side * a + b : side * a + b + 1, :] = jnp.sum(
                    tap_rows, axis=0, keepdims=True
                )
        grad_in = mm(us[l], da, ((0,), (0,)))
        grad_out = mm(gs[l], d_rows, ((0,), (0,)))

        part[l, 0:128] = jnp.concatenate([grad_in[:, :128], grad_in[:, 128:]], axis=0).astype(bf16)
        part[l, 128:256] = packed(grad_out).astype(bf16)
        tap_sums = dk_ref[...]
        high = tap_sums.astype(bf16)
        low = (tap_sums - high.astype(f32)).astype(bf16)
        turn = tap_perm_ref[...]
        part[l, 256:320] = (mm(turn, high, ((0,), (0,))) + mm(turn, low, ((0,), (0,)))).astype(bf16)

        @pl.when(sec != mine)
        def _():
            part_copy(l, sec, mine).start()

        for copy in sent:
            copy.wait_recv()
        base = grad[...].reshape(16, 8, 128)
        slot = layers + l
        top_part = base[0:3] + rows_in[slot, 0].astype(f32).reshape(4, 8, 128)[1:4]
        bottom_part = base[13:16] + rows_in[slot, 1].astype(f32).reshape(4, 8, 128)[0:3]
        field[...] = jnp.concatenate([top_part, base[3:13], bottom_part], axis=0).reshape(128, 128)
        for edge in range(2):
            sides = edge_in[slot, edge].astype(f32)
            upper = corner_in[slot, edge, 0].astype(f32)
            lower = corner_in[slot, edge, 1].astype(f32)
            for pair in range(2):
                place = (0 if edge == WEST else 6) + pair
                corners = [upper[8 * pair : 8 * pair + 8], lower[8 * pair : 8 * pair + 8]]
                extra = sides[16 * pair : 16 * pair + 16] + jnp.concatenate(corners, axis=0)
                field[pl.ds(place, 16, stride=8), :] = (
                    field[pl.ds(place, 16, stride=8), :] + extra
                )
        result = field[...].astype(bf16)
        grad[...] = result.astype(f32)

        @pl.when(block == 0)
        def _():
            gst[sec] = restored(result)

        @pl.when((block == 0) & (sec != mine))
        def _():
            g_copy(sec, mine).start()

        for copy in sent:
            copy.wait_send()
        return carry

    lax.fori_loop(0, layers, backward_step, 0)

    for i in range(blocks):
        total = part[mine * blocks + i].astype(f32)
        for other in others:
            part_copy(mine * blocks + i, mine, other).wait_recv()
            total = total + arec[other, i].astype(f32)
        total_ref[320 * i : 320 * i + 320] = total.astype(bf16)

    def place(tile):
        return pl.ds(pl.multiple_of(tile * piece, 16), piece)

    def ahead(j):
        return lax.rem(me + j, tile_count)

    def behind(j):
        return lax.rem(me + tile_count - j, tile_count)

    def scatter(j, tile):
        return across("tile", tile, total_ref.at[place(tile)], rs.at[j], rsend.at[j], rrecv.at[j])

    def spread(j, tile, source):
        spot = place(source)
        return across("tile", tile, fin.at[spot], fin.at[spot], csend.at[j], crecv.at[j])

    def each(body):
        def step(j, carry):
            body(j)
            return carry

        lax.fori_loop(1, tile_count, step, 0)

    each(lambda j: scatter(j, ahead(j)).start())

    def gathered(j, total):
        scatter(j, ahead(j)).wait_recv()
        return total + rs[j].astype(f32)

    total = lax.fori_loop(1, tile_count, gathered, total_ref[place(me)].astype(f32))
    fin[place(me)] = (total * grad_scale).astype(bf16)
    each(lambda j: spread(j, ahead(j), me).start())

    zo_ref[0, mine, 0] = zst[mine]
    go_ref[0, mine, 0] = gst[mine]
    for other in others:
        z_copy(mine, other).wait_recv()
        zo_ref[0, other, 0] = zrec[other]
        g_copy(mine, other).wait_recv()
        go_ref[0, other, 0] = grec[other]
    for other in others:
        for copy in weight_copies(other, mine):
            copy.wait_send()
        z_copy(other, mine).wait_send()
        g_copy(other, mine).wait_send()
        for i in range(blocks):
            part_copy(other * blocks + i, other, mine).wait_send()
    each(lambda j: scatter(j, ahead(j)).wait_send())
    each(lambda j: spread(j, me, behind(j)).wait_recv())
    each(lambda j: spread(j, ahead(j), me).wait_send())
    for i in range(blocks):
        whole = fin[320 * i : 320 * i + 320].astype(f32)
        dw1_out[i] = jnp.concatenate([whole[0:64], whole[64:128]], axis=1)
        dw2_out[i] = unpacked(whole[128:256])
        dk_out[i] = whole[256:305, :64] + whole[256:305, 64:]


def on_device(inputs, cotangent, depth_weight, in_weight, out_weight, neighbours, orientation):
    micro_count, _, extent, merged = inputs.shape
    blocks, taps, channels = depth_weight.shape
    hidden = in_weight.shape[2]
    tile_count = lax.axis_size("tile")
    sections = lax.axis_size("section")
    layers = blocks * sections
    grad_scale = 1.0 / math.sqrt(micro_count * tile_count * extent * extent)
    piece = -(-320 * blocks // (16 * tile_count)) * 16

    vmem = pl.BlockSpec(memory_space=pltpu.VMEM)
    smem = pl.BlockSpec(memory_space=pltpu.SMEM)
    zo, go, dk, dw1, dw2 = pl.pallas_call(
        functools.partial(kernel, tile_count, sections, blocks, piece, grad_scale),
        out_shape=(
            jax.ShapeDtypeStruct((1, micro_count, 1, extent, merged), bf16),
            jax.ShapeDtypeStruct((1, micro_count, 1, extent, merged), bf16),
            jax.ShapeDtypeStruct((blocks, taps, channels), f32),
            jax.ShapeDtypeStruct((blocks, channels, hidden), f32),
            jax.ShapeDtypeStruct((blocks, hidden, channels), f32),
        ),
        in_specs=[vmem] * 5 + [smem] * 2,
        out_specs=(vmem,) * 5,
        scratch_shapes=[
            pltpu.VMEM((2, 22, 128), f32),
            pltpu.VMEM((256, 256), bf16),
            pltpu.VMEM((64, 64), bf16),
            pltpu.VMEM((2, 3, 32, 128), f32),
            pltpu.VMEM((sections, blocks, 64, 128), bf16),
            pltpu.VMEM((layers, 64, 128), f32),
            pltpu.VMEM((sections, blocks, channels, hidden), bf16),
            pltpu.VMEM((sections, blocks, hidden, channels), bf16),
            pltpu.VMEM((sections, 16, 1024), bf16),
            pltpu.VMEM((sections, 16, 1024), bf16),
            pltpu.VMEM((sections, 16, 1024), bf16),
            pltpu.VMEM((sections, 16, 1024), bf16),
            pltpu.VMEM((128, 128), f32),
            pltpu.VMEM((64, 128), f32),
            pltpu.VMEM((layers, 320, 128), bf16),
            pltpu.VMEM((sections, blocks, 320, 128), bf16),
            pltpu.VMEM((piece * tile_count, 128), bf16),
            pltpu.VMEM((tile_count, piece, 128), bf16),
            pltpu.VMEM((piece * tile_count, 128), bf16),
            pltpu.VMEM((layers, 22, 24, 128), f32),
            pltpu.VMEM((layers, 22, 16, 128), f32),
            pltpu.VMEM((2, 32, 128), bf16),
            pltpu.VMEM((2, 32, 128), bf16),
            pltpu.VMEM((2, 2, 16, 128), bf16),
            pltpu.VMEM((2 * layers, 2, 32, 128), bf16),
            pltpu.VMEM((2 * layers, 2, 32, 128), bf16),
            pltpu.VMEM((2 * layers, 2, 2, 16, 128), bf16),
            pltpu.VMEM((2, 2, 32, 128), f32),
            pltpu.VMEM((layers, 128, 128), f32),
            pltpu.VMEM((layers, 128, 128), f32),
            pltpu.VMEM((layers, 256, 64), bf16),
            pltpu.VMEM((layers, 256, 256), bf16),
            pltpu.VMEM((layers, 256, 256), f32),
            pltpu.VMEM((28, 24, 128), f32),
            pltpu.VMEM((28, 24, 128), f32),
            pltpu.VMEM((22, 24, 128), f32),
            pltpu.VMEM((2, 2, 32, 128), f32),
            pltpu.VMEM((128, 128), f32),
            pltpu.VMEM((128, 128), f32),
            pltpu.VMEM((256, 128), bf16),
            pltpu.SemaphoreType.DMA((8,)),
            pltpu.SemaphoreType.DMA((layers, 8)),
            pltpu.SemaphoreType.DMA((layers, 8)),
            pltpu.SemaphoreType.DMA((sections, 3)),
            pltpu.SemaphoreType.DMA((sections, 3)),
            pltpu.SemaphoreType.DMA((sections,)),
            pltpu.SemaphoreType.DMA((sections,)),
            pltpu.SemaphoreType.DMA((sections,)),
            pltpu.SemaphoreType.DMA((sections,)),
            pltpu.SemaphoreType.DMA((layers,)),
            pltpu.SemaphoreType.DMA((sections, blocks)),
            pltpu.SemaphoreType.DMA((tile_count,)),
            pltpu.SemaphoreType.DMA((tile_count,)),
            pltpu.SemaphoreType.DMA((tile_count,)),
            pltpu.SemaphoreType.DMA((tile_count,)),
        ],
        compiler_params=pltpu.CompilerParams(
            collective_id=0, has_side_effects=True, vmem_limit_bytes=40 * 1024 * 1024
        ),
    )(inputs, cotangent, depth_weight, in_weight, out_weight, neighbours, orientation)
    return (zo, go, dk, dw1, dw2)


def solution(mesh):
    in_specs = (
        P(None, "tile", None, None),
        P(None, "tile", None, None),
        P("section", None, None),
        P("section", None, None),
        P("section", None, None),
        P("tile", None),
        P(),
    )
    out_specs = (
        P("section", None, "tile", None, None),
        P("section", None, "tile", None, None),
        P("section", None, None),
        P("section", None, None),
        P("section", None, None),
    )
    return jax.shard_map(
        on_device, mesh=mesh, in_specs=in_specs, out_specs=out_specs, check_vma=False
    )
```
